512 devices in a mesh: sim: 32 (over z_lo, y, core), grp: 4 (over z_hi), gz: 4 (over x).
Axes of the slice: x: 4, y: 4, z: 16 (z_hi: 4, z_lo: 4; z = z_hi * 4 + z_lo), core: 2. Of those that a mesh axis runs over, the one named last changes fastest.
Arguments:
- fields: float32 [8, 2, 1024, 1024], P(None, None, 'sim', ('grp', 'gz')), may hold values from -6 to 6
- diffusivity: float32 [8], replicated, may hold values from 0.03 to 0.12
- velocity: float32 [2, 8], replicated, may hold values from -0.4 to 0.4
- coupling: float32 [8, 8], replicated, may hold values from -0.6 to 0.6
- basis_x: bfloat16 [1024, 128], replicated, may hold values from -0.1875 to 0.1875
- basis_y: bfloat16 [1024, 128], replicated, may hold values from -0.1875 to 0.1875
Outputs:
- fields_out: float32 [8, 2, 1024, 1024], P(None, None, 'sim', ('grp', 'gz'))
- gram_x: float32 [1024, 1024], P('sim', ('grp', 'gz'))
- gram_y: float32 [1024, 1024], P(('grp', 'gz'), 'sim')
- core: float32 [8, 2, 128, 128], P(None, None, 'sim', ('grp', 'gz'))
The draws below stay inside these ranges and needn't reach their ends.
All inputs are finite; a program needn't handle non-finite values.
Results may differ from the reference program's by a relative error of at most 0.0003.
Values sent between devices are 32-bit elements; how exact they have to be, the bound alone decides.
A program may use at most 64 MiB of HBM per device.

```python
import jax
import jax.numpy as jnp
from jax import lax

FIELDS = 8
NX = 1024
NY = 1024
RANK = 128
NZ = 2
STEPS = 2


def levels(own_key, shape, pieces, smallest, largest):
    def one(dim, parts):
        heights = jax.random.uniform(jax.random.fold_in(jax.random.fold_in(own_key, 6), dim), (parts,), jnp.float32, smallest / len(pieces), largest / len(pieces))
        return jnp.repeat(jnp.exp(heights), shape[dim] // parts).reshape((-1,) + (1,) * (len(shape) - dim - 1))

    loudness = one(*pieces[0])
    for cut in pieces[1:]:
        loudness = loudness * one(*cut)
    return loudness


def gaussian(rng, dims, spread, most, cuts=(), held_as=jnp.bfloat16):
    gain = levels(rng, dims, cuts, -0.22, 0.18) if cuts else 1.0
    result = jax.random.normal(rng, dims, jnp.float32) * spread * gain
    return jnp.minimum(jnp.maximum(result, -most), most).astype(held_as)


def setup_inputs(seed: int = 0) -> dict:
    key_list = jax.random.split(jax.random.key(seed), 7)
    fields = gaussian(key_list[0], (FIELDS, NZ, NX, NY), 1.0, 6.0, ((2, 32), (3, 16)), jnp.float32)
    diffusivity = jnp.clip(jax.random.uniform(key_list[1], (FIELDS,), jnp.float32, 0.03, 0.12), 0.03, 0.12)
    velocity = jnp.clip(jax.random.uniform(key_list[2], (2, FIELDS), jnp.float32, -0.4, 0.4), -0.4, 0.4)
    coupling = gaussian(key_list[3], (FIELDS, FIELDS), 0.15, 0.6, (), jnp.float32)
    basis_x = gaussian(key_list[4], (NX, RANK), NX ** -0.5, 0.1875)
    basis_y = gaussian(key_list[5], (NY, RANK), NY ** -0.5, 0.1875)
    return dict(fields=fields, diffusivity=diffusivity, velocity=velocity, coupling=coupling, basis_x=basis_x, basis_y=basis_y)


time_step = 1.0


def rates(state, diffusivity, velocity, coupling):
    lapl = -6.0 * state
    for axis_id in (1, 2, 3):
        lapl = lapl + jnp.roll(state, 1, axis_id) + jnp.roll(state, -1, axis_id)
    grad_x = (jnp.roll(state, -1, 2) - jnp.roll(state, 1, 2)) * 0.5
    grad_y = (jnp.roll(state, -1, 3) - jnp.roll(state, 1, 3)) * 0.5
    react = jnp.einsum("fg,gzxy->fzxy", coupling, jnp.tanh(state), precision=lax.Precision.HIGHEST)
    return (diffusivity[:, None, None, None] * lapl
            - velocity[0][:, None, None, None] * grad_x
            - velocity[1][:, None, None, None] * grad_y + react)


def reference(fields, diffusivity, velocity, coupling, basis_x, basis_y):
    state = fields
    for repeat in range(STEPS):
        first = rates(state, diffusivity, velocity, coupling)
        second = rates(state + 0.5 * time_step * first, diffusivity, velocity, coupling)
        third = rates(state + 0.5 * time_step * second, diffusivity, velocity, coupling)
        fourth = rates(state + time_step * third, diffusivity, velocity, coupling)
        state = state + (time_step / 6.0) * (first + 2.0 * second + 2.0 * third + fourth)
    unfold_x = jnp.transpose(state, (2, 0, 1, 3)).reshape(NX, -1)
    gram_x = jnp.dot(unfold_x, unfold_x.T, precision=lax.Precision.HIGHEST) / (FIELDS * NZ * NY)
    projected = jnp.einsum("xr,fzxy->fzry", basis_x.astype(jnp.float32), state, precision=lax.Precision.HIGHEST)
    unfold_y = jnp.transpose(projected, (3, 0, 1, 2)).reshape(NY, -1)
    gram_y = jnp.dot(unfold_y, unfold_y.T, precision=lax.Precision.HIGHEST) / (FIELDS * NZ * RANK)
    core = jnp.einsum("ys,fzry->fzrs", basis_y.astype(jnp.float32), projected, precision=lax.Precision.HIGHEST)
    return state, gram_x, gram_y, core
```

```python
import functools

import jax
import jax.numpy as jnp
from jax import lax
from jax.experimental import pallas as pl
from jax.experimental.pallas import tpu as pltpu
from jax.sharding import PartitionSpec as P

NF = 8
NX = 1024
NY = 1024
RANK = 128
NZ = 2
STEPS = 2
Q = 4
XR = 32
YC = 64
HALO = 8
ROWS = XR + 2 * HALO
LANES = 128
HF = NF // 2
MESH = pl.DeviceIdType.MESH
F32 = jnp.float32
BF16 = jnp.bfloat16


def split(a):
    hi = a.astype(BF16)
    lo = (a - hi.astype(F32)).astype(BF16)
    return hi, lo


def dot(a, b, dims):
    return lax.dot_general(a, b, (dims, ((), ())), preferred_element_type=F32)


def dot3(a, b, dims):
    ah, al = split(a)
    bh, bl = split(b)
    return dot(ah, bh, dims) + (dot(ah, bl, dims) + dot(al, bh, dims))


NN = ((1,), (0,))
NT = ((1,), (1,))


def kernel(
    u_ref, diff_ref, vel_ref, coup_ref, bx_ref, by_ref,
    uo_ref, gx_ref, gy_ref, core_ref,
    w, el, er, hl, hr, v, base, acc, th,
    a_ref, gyb, gzb, ct, ra, pbx, rb, pf, rp, pd, gh, gxb, ds, rd, pby, rdb, cot, rc, et, bxt, byt,
    s_halo, r_halo, s_yc, r_yc, s_zc, r_zc, s_pz, r_pz, s_zh, r_zh, s_px, r_px,
    s_ra, r_ra, s_rb, r_rb, s_rd, r_rd, s_rdb, r_rdb, s_co, r_co,
):
    sim = lax.axis_index("sim")
    zh = lax.axis_index("grp")
    x = lax.axis_index("gz")
    zl = sim // (2 * Q)
    y = (sim // 2) % Q
    c = sim % 2
    nsim = 2 * Q * Q
    nblk = Q * Q
    blk = zh * Q + x

    def dev(zl_, y_, c_, zh_, x_):
        return (zl_ * (2 * Q) + y_ * 2 + c_, zh_, x_)

    def cyc(i, d):
        return (i + d + Q) % Q

    def halo_dev(dx, dy):
        b = (blk + dy + nblk) % nblk
        return ((sim + dx + nsim) % nsim, b // Q, b % Q)

    pairs = [(d, e) for d in range(Q) for e in range(2) if (d, e) != (0, 0)]
    self_b = zl == zh
    self_d = (x == y) & (c == zl // 2)

    barrier = pltpu.get_barrier_semaphore()

    def tell(d):
        pl.semaphore_signal(barrier, inc=1, device_id=d, device_id_type=MESH)

    halo_dirs = [(dx, dy) for dx in (-1, 0, 1) for dy in (-1, 0, 1) if (dx, dy) != (0, 0)]
    for dx, dy in halo_dirs:
        tell(halo_dev(dx, dy))
    for d, e in pairs:
        tell(dev(zl, cyc(y, -d), c ^ e, zh, x))
        tell(dev(zl, y, c ^ e, zh, cyc(x, -d)))
        if d:
            tell(dev(cyc(zl, -d), y, c ^ e, zh, x))
    for d in range(1, Q):
        tell(dev(zl, y, c, cyc(zh, -d), x))
    for k in range(Q):
        @pl.when(~(self_b & (k == zh)))
        def _():
            tell(dev(zh, y, c, k, x))

        @pl.when(~(self_d & (k == zl)))
        def _():
            tell(dev(k, x, zl // 2, zh, y))

    sends = []

    def send(src, dst, ssem, rsem, target):
        copy = pltpu.make_async_remote_copy(
            src_ref=src, dst_ref=dst, send_sem=ssem, recv_sem=rsem, device_id=target, device_id_type=MESH
        )
        copy.start()
        sends.append(copy)

    def arrive(dst, ssem, rsem, source):
        pltpu.make_async_remote_copy(
            src_ref=dst, dst_ref=dst, send_sem=ssem, recv_sem=rsem, device_id=source, device_id_type=MESH
        ).wait_recv()

    def lane(shape):
        return lax.broadcasted_iota(jnp.int32, shape, len(shape) - 1)

    zero = jnp.zeros((XR, LANES), F32)
    lane32 = lane((XR, LANES))
    left = zero
    right = zero
    for fz in range(NF * NZ):
        w[fz, 0:XR, :] = zero
        w[fz, 0:XR, 0:YC] = u_ref[fz // NZ, fz % NZ]
    for fz in range(NF * NZ):
        own = w[fz, 0:XR, :]
        here = lane32 // HALO == fz
        left = jnp.where(here, pltpu.roll(own, fz * HALO, 1) if fz else own, left)
        right = jnp.where(here, pltpu.roll(own, (fz * HALO - (YC - HALO)) % LANES, 1) if fz != 7 else own, right)
    el[...] = left
    er[...] = right

    out_count = jnp.int32(8 + 7 + 6 + 3 + 7 + 2 * Q) - self_b.astype(jnp.int32) - self_d.astype(jnp.int32)
    pl.semaphore_wait(barrier, out_count)

    def halo_sem(dx, dy):
        return (dx + 1) * 3 + dy + 1

    top, bottom = pl.ds(0, HALO), pl.ds(XR - HALO, HALO)
    below, above, mine = pl.ds(XR, HALO), pl.ds(XR + HALO, HALO), pl.ds(0, XR)
    halo_plan = [
        (-1, 0, w.at[:, top], w.at[:, below]),
        (1, 0, w.at[:, bottom], w.at[:, above]),
        (0, -1, el, hr.at[mine]),
        (0, 1, er, hl.at[mine]),
        (-1, -1, el.at[top], hr.at[below]),
        (1, -1, el.at[bottom], hr.at[above]),
        (-1, 1, er.at[top], hl.at[below]),
        (1, 1, er.at[bottom], hl.at[above]),
    ]
    for dx, dy, src, dst in halo_plan:
        i = halo_sem(dx, dy)
        send(src, dst, s_halo.at[i], r_halo.at[i], halo_dev(dx, dy))

    bxt[...] = bx_ref[pl.ds(pl.multiple_of(zl * 256, 256), 256), :].astype(F32).T.astype(BF16)
    byt[...] = jnp.concatenate(
        [by_ref[pl.ds(pl.multiple_of((k * Q + x) * YC, YC), YC), :].astype(F32) for k in range(Q)], axis=0
    ).T.astype(BF16)

    for dx, dy, src, dst in halo_plan:
        i = halo_sem(dx, dy)
        arrive(dst, s_halo.at[i], r_halo.at[i], halo_dev(-dx, -dy))

    lane48 = lane((ROWS, LANES))
    is_right = (lane48 >= YC) & (lane48 < YC + HALO)
    is_left = lane48 >= LANES - HALO
    for fz in range(NF * NZ):
        from_left = pltpu.roll(hl[...], (LANES - HALO - fz * HALO) % LANES, 1) if fz != 15 else hl[...]
        from_right = pltpu.roll(hr[...], (YC - fz * HALO) % LANES, 1) if fz != 8 else hr[...]
        full = jnp.where(is_left, from_left, jnp.where(is_right, from_right, w[fz]))
        v[fz // NZ, fz % NZ] = full
        base[fz // NZ, fz % NZ] = full
        th[0, fz // NZ, fz % NZ] = jnp.tanh(full)

    def step(_, carry):
        for stage in range(4):
            now, later = stage % 2, (stage + 1) % 2

            def field(f, carry2):
                d = diff_ref[f]
                vx = vel_ref[0, f] * 0.5
                vy = vel_ref[1, f] * 0.5
                for z in range(NZ):
                    s = v[f, z]
                    k = th[now, 0, z] * coup_ref[f, 0]
                    for g in range(1, NF):
                        k = k + th[now, g, z] * coup_ref[f, g]
                    k = k + s * (-6.0 * d) + pltpu.roll(s, ROWS - 1, 0) * (d - vx) + pltpu.roll(s, 1, 0) * (d + vx)
                    k = k + pltpu.roll(s, LANES - 1, 1) * (d - vy) + pltpu.roll(s, 1, 1) * (d + vy)
                    if z == 0:
                        first = k + v[f, 1] * (2.0 * d)
                        s0 = s
                    else:
                        second = k + s0 * (2.0 * d)
                for z, k in ((0, first), (1, second)):
                    if stage == 0:
                        acc[f, z] = k
                        new = base[f, z] + 0.5 * k
                    elif stage == 1:
                        acc[f, z] = acc[f, z] + 2.0 * k
                        new = base[f, z] + 0.5 * k
                    elif stage == 2:
                        acc[f, z] = acc[f, z] + 2.0 * k
                        new = base[f, z] + k
                    else:
                        new = base[f, z] + (acc[f, z] + k) * (1.0 / 6.0)
                        base[f, z] = new
                    v[f, z] = new
                    th[later, f, z] = jnp.tanh(new)
                return carry2

            lax.fori_loop(0, NF, field, 0)
        return carry

    lax.fori_loop(0, STEPS, step, 0)

    low32 = lane32 < YC
    for f in range(NF):
        a_ref[f] = jnp.where(low32, base[f, 0, 0:XR, :], pltpu.roll(base[f, 1, 0:XR, :], YC, 1))

    me_yc = y * 2 + c
    me_zc = c * Q + zl
    for d, e in pairs:
        ty, tc = cyc(y, d), c ^ e
        send(a_ref.at[pl.ds(tc * HF, HF)], gyb.at[me_yc], s_yc.at[d * 2 + e], r_yc.at[me_yc], dev(zl, ty, tc, zh, x))
    for d, e in pairs:
        if d:
            tz, tc = cyc(zl, d), c ^ e
            send(a_ref.at[pl.ds(tc * HF, HF)], gzb.at[me_zc], s_zc.at[d * 2 + e], r_zc.at[me_zc], dev(tz, y, tc, zh, x))
    for f in range(NF):
        for z in range(NZ):
            uo_ref[f, z] = base[f, z, 0:XR, 0:YC]
    gyb[me_yc] = a_ref[pl.ds(c * HF, HF)]

    for d, e in pairs:
        sy, sc = cyc(y, -d), c ^ e
        i = sy * 2 + sc
        arrive(gyb.at[i], s_yc.at[d * 2 + e], r_yc.at[i], dev(zl, sy, sc, zh, x))

    def wide(ref):
        return jnp.concatenate([ref[:, f].reshape(2 * Q * XR, LANES) for f in range(HF)], axis=1)

    gyw = wide(gyb)
    gyh, gyl = split(gyw)
    part = dot(bxt[...], gyh, NN) + dot(bxt[...], gyl, NN)
    for f in range(HF):
        pf[f] = part[:, f * LANES:(f + 1) * LANES]

    def rank_rows(z_):
        return pl.ds(pl.multiple_of(z_ * 32 + y * 8, 8), 8)

    for d in range(1, Q):
        tz = cyc(zl, d)
        send(pf.at[:, rank_rows(tz)], rp.at[zl], s_pz.at[d], r_pz.at[zl], dev(tz, y, c, zh, x))
    rp[zl] = pf[:, rank_rows(zl), :]
    for e in range(2):
        gzb[e * Q + zl] = gyb[y * 2 + e]

    for d, e in pairs:
        if d:
            sz, sc = cyc(zl, -d), c ^ e
            i = sc * Q + sz
            arrive(gzb.at[i], s_zc.at[d * 2 + e], r_zc.at[i], dev(sz, y, sc, zh, x))
    gzh, gzl = split(wide(gzb))
    block = dot(gyh, gzh, NT) + (dot(gyh, gzl, NT) + dot(gyl, gzh, NT))
    for k in range(Q):
        for e in range(2):
            ct[k, e] = block[k * YC:(k + 1) * YC, e * LANES:(e + 1) * LANES]
    me_xc = x * 2 + c
    for d, e in pairs:
        tx, tc = cyc(x, d), c ^ e
        send(ct.at[tx, tc], ra.at[me_xc], s_ra.at[d * 2 + e], r_ra.at[me_xc], dev(zl, y, tc, zh, tx))
    ra[me_xc] = ct[x, c]

    for d in range(1, Q):
        sz = cyc(zl, -d)
        arrive(rp.at[sz], s_pz.at[d], r_pz.at[sz], dev(sz, y, c, zh, x))
    own = (rp[0] + rp[1]) + (rp[2] + rp[3])
    pd[...] = own
    for d in range(1, Q):
        th_ = cyc(zh, d)
        send(pd, gh.at[zh], s_zh.at[d], r_zh.at[zh], dev(zl, y, c, th_, x))
    for d in range(1, Q):
        tx = cyc(x, d)
        send(pd, gxb.at[x], s_px.at[d], r_px.at[x], dev(zl, y, c, zh, tx))
    gh[zh] = own
    gxb[x] = own

    for d, e in pairs:
        sx, sc = cyc(x, -d), c ^ e
        i = sx * 2 + sc
        arrive(ra.at[i], s_ra.at[d * 2 + e], r_ra.at[i], dev(zl, y, sc, zh, sx))
    total = ra[0]
    for i in range(1, 2 * Q):
        total = total + ra[i]
    turned = jnp.concatenate([total, total], axis=0).T
    low16 = lane((16, LANES)) < YC
    late = []
    for k in range(Q):
        pbx[k] = jnp.where(low16, turned[k * 32:k * 32 + 16], turned[k * 32 + 16:k * 32 + 32])
        same = self_b & (k == zl)
        copy = pltpu.make_async_remote_copy(
            src_ref=pbx.at[k], dst_ref=rb.at[zh], send_sem=s_rb.at[k], recv_sem=r_rb.at[zh],
            device_id=dev(k, y, c, zl, x), device_id_type=MESH,
        )
        late.append((same, copy))

        @pl.when(same)
        def _():
            rb[zh] = pbx[k]

        @pl.when(~same)
        def _():
            copy.start()

    for d in range(1, Q):
        sh = cyc(zh, -d)
        arrive(gh.at[sh], s_zh.at[d], r_zh.at[sh], dev(zl, y, c, sh, x))
    low = lane((32, LANES)) < YC

    def unpack(ref):
        g = [ref[k].reshape(32, LANES) for k in range(Q)]
        r = [pltpu.roll(t, YC, 1) for t in g]
        first = jnp.concatenate([jnp.where(low, g[0], r[1]), jnp.where(low, g[2], r[3])], axis=1)
        second = jnp.concatenate([jnp.where(low, r[0], g[1]), jnp.where(low, r[2], g[3])], axis=1)
        return jnp.concatenate([first, second], axis=0)

    cols = unpack(gh)
    ch, cl = split(cols)
    two_h = jnp.concatenate([ch, ch], axis=0)
    two_l = jnp.concatenate([cl, cl], axis=0)
    cot[...] = dot(byt[...], two_h, NT) + dot(byt[...], two_l, NT)

    def core_rows(x_):
        return pl.ds(pl.multiple_of(zh * 32 + x_ * 8, 8), 8)

    for d, e in pairs:
        tx, tc = cyc(x, d), c ^ e
        send(cot.at[core_rows(tx)], rc.at[me_xc], s_co.at[d * 2 + e], r_co.at[me_xc], dev(zl, y, tc, zh, tx))
    rc[me_xc] = cot[core_rows(x), :]

    for d in range(1, Q):
        sx = cyc(x, -d)
        arrive(gxb.at[sx], s_px.at[d], r_px.at[sx], dev(zl, y, c, zh, sx))
    rh, rl = split(unpack(gxb).T)
    dd = dot(rh, ch, NN) + (dot(rh, cl, NN) + dot(rl, ch, NN))
    for k in range(Q):
        for e in range(2):
            ds[k, e] = dd[k * YC:(k + 1) * YC, e * LANES:(e + 1) * LANES]
    for d, e in pairs:
        ty, tc = cyc(y, d), c ^ e
        send(ds.at[ty, tc], rd.at[me_yc], s_rd.at[d * 2 + e], r_rd.at[me_yc], dev(zl, ty, tc, zh, x))
    rd[me_yc] = ds[y, c]

    for k in range(Q):
        @pl.when(~(self_b & (k == zh)))
        def _():
            arrive(rb.at[k], s_rb.at[k], r_rb.at[k], dev(zh, y, c, k, x))
    gsum = ((rb[0] + rb[1]) + (rb[2] + rb[3])) * (1.0 / (NF * NZ * NY))
    gx_ref[0:16, :] = gsum[:, 0:YC]
    gx_ref[16:32, :] = pltpu.roll(gsum, YC, 1)[:, 0:YC]

    for d, e in pairs:
        sy, sc = cyc(y, -d), c ^ e
        i = sy * 2 + sc
        arrive(rd.at[i], s_rd.at[d * 2 + e], r_rd.at[i], dev(zl, sy, sc, zh, x))
    total = rd[0]
    for i in range(1, 2 * Q):
        total = total + rd[i]
    lane16 = lane((16, LANES))
    for k in range(2):
        for h in range(2):
            packed = jnp.zeros((16, LANES), F32)
            for j in range(4):
                piece = total[j * 16:(j + 1) * 16]
                shift = (j * 32 - k * 64 - h * 32) % LANES
                piece = pltpu.roll(piece, shift, 1) if shift else piece
                packed = jnp.where(lane16 // 32 == j, piece, packed)
            m = k * 2 + h
            pby[m] = packed
            same = self_d & (2 * c + k == zl) & (c == h)
            copy = pltpu.make_async_remote_copy(
                src_ref=pby.at[m], dst_ref=rdb.at[zl], send_sem=s_rdb.at[m], recv_sem=r_rdb.at[zl],
                device_id=dev(2 * c + k, x, h, zh, y), device_id_type=MESH,
            )
            late.append((same, copy))

            @pl.when(same)
            def _():
                rdb[zl] = pby[m]

            @pl.when(~same)
            def _():
                copy.start()

    for d, e in pairs:
        sx, sc = cyc(x, -d), c ^ e
        i = sx * 2 + sc
        arrive(rc.at[i], s_co.at[d * 2 + e], r_co.at[i], dev(zl, y, sc, zh, sx))
    e0 = (rc[0] + rc[2]) + (rc[4] + rc[6])
    e1 = (rc[1] + rc[3]) + (rc[5] + rc[7])
    both = jnp.where(lane((8, LANES)) < 64, e0, e1)
    et[...] = jnp.concatenate([both] * 16, axis=0).T
    for fh in range(2):
        for z in range(NZ):
            for f in range(HF):
                at = fh * 64 + z * 32 + f * 8
                core_ref[fh * HF + f, z] = jnp.where(c == 0, et[at:at + 4, 0:8], et[at + 4:at + 8, 0:8])

    for k in range(Q):
        @pl.when(~(self_d & (k == zl)))
        def _():
            arrive(rdb.at[k], s_rdb.at[k], r_rdb.at[k], dev(k, x, zl // 2, zh, y))
    gsum = ((rdb[0] + rdb[1]) + (rdb[2] + rdb[3])) * (1.0 / (NF * NZ * RANK))
    for j in range(4):
        gy_ref[j * 16:(j + 1) * 16, :] = (pltpu.roll(gsum, LANES - j * 32, 1) if j else gsum)[:, 0:32]

    for copy in sends:
        copy.wait_send()
    for same, copy in late:
        @pl.when(~same)
        def _():
            copy.wait_send()


def shards(fields, diffusivity, velocity, coupling, basis_x, basis_y):
    vm = lambda *shape: pltpu.VMEM(shape, F32)
    dma = lambda n: pltpu.SemaphoreType.DMA((n,))
    vspec = pl.BlockSpec(memory_space=pltpu.VMEM)
    sspec = pl.BlockSpec(memory_space=pltpu.SMEM)
    scratch = [
        vm(NF * NZ, ROWS, LANES), vm(XR, LANES), vm(XR, LANES), vm(ROWS, LANES), vm(ROWS, LANES),
        vm(NF, NZ, ROWS, LANES), vm(NF, NZ, ROWS, LANES), vm(NF, NZ, ROWS, LANES), vm(2, NF, NZ, ROWS, LANES),
        vm(NF, XR, LANES),
        vm(2 * Q, HF, XR, LANES), vm(2 * Q, HF, XR, LANES),
        vm(Q, 2, YC, LANES), vm(2 * Q, YC, LANES), vm(Q, 16, LANES), vm(Q, 16, LANES),
        vm(HF, RANK, LANES), vm(Q, HF, 8, LANES), vm(HF, 8, LANES),
        vm(Q, HF, 8, LANES), vm(Q, HF, 8, LANES),
        vm(Q, 2, YC, LANES), vm(2 * Q, YC, LANES), vm(Q, 16, LANES), vm(Q, 16, LANES),
        vm(RANK, LANES), vm(2 * Q, 8, LANES), vm(LANES, LANES),
        pltpu.VMEM((RANK, 256), BF16), pltpu.VMEM((RANK, 256), BF16),
        dma(9), dma(9), dma(8), dma(8), dma(8), dma(8), dma(4), dma(4), dma(4), dma(4), dma(4), dma(4),
        dma(8), dma(8), dma(4), dma(4), dma(8), dma(8), dma(4), dma(4), dma(8), dma(8),
    ]
    return pl.pallas_call(
        kernel,
        out_shape=(
            jax.ShapeDtypeStruct((NF, NZ, XR, YC), F32),
            jax.ShapeDtypeStruct((XR, YC), F32),
            jax.ShapeDtypeStruct((YC, XR), F32),
            jax.ShapeDtypeStruct((NF, NZ, 4, 8), F32),
        ),
        in_specs=[vspec, sspec, sspec, sspec, vspec, vspec],
        out_specs=(vspec, vspec, vspec, vspec),
        scratch_shapes=scratch,
        compiler_params=pltpu.CompilerParams(
            collective_id=0, has_side_effects=True, vmem_limit_bytes=40 * 1024 * 1024
        ),
    )(fields, diffusivity, velocity, coupling, basis_x, basis_y)


def solution(mesh):
    in_specs = (P(None, None, "sim", ("grp", "gz")), P(), P(), P(), P(), P())
    out_specs = (
        P(None, None, "sim", ("grp", "gz")),
        P("sim", ("grp", "gz")),
        P(("grp", "gz"), "sim"),
        P(None, None, "sim", ("grp", "gz")),
    )
    return jax.shard_map(shards, mesh=mesh, in_specs=in_specs, out_specs=out_specs, check_vma=False)
```

```python
import functools

import jax
import jax.numpy as jnp
from jax import lax
from jax.experimental import pallas as pl
from jax.experimental.pallas import tpu as pltpu
from jax.sharding import PartitionSpec as P

NF = 8
NX = 1024
NY = 1024
RANK = 128
NZ = 2
STEPS = 2
Q = 4
XR = 32
YC = 64
HALO = 8
ROWS = XR + 2 * HALO
LANES = 128
HF = NF // 2
MESH = pl.DeviceIdType.MESH
F32 = jnp.float32
BF16 = jnp.bfloat16


def split(a):
    hi = a.astype(BF16)
    lo = (a - hi.astype(F32)).astype(BF16)
    return hi, lo


def dot(a, b, dims):
    return lax.dot_general(a, b, (dims, ((), ())), preferred_element_type=F32)


def dot3(a, b, dims):
    ah, al = split(a)
    bh, bl = split(b)
    return dot(ah, bh, dims) + (dot(ah, bl, dims) + dot(al, bh, dims))


NN = ((1,), (0,))
NT = ((1,), (1,))


def kernel(
    u_hbm, diff_hbm, vel_hbm, coup_hbm, bx_hbm, by_hbm,
    uo_hbm, gx_hbm, gy_hbm, core_hbm,
    uo_ref, gx_ref, gy_ref, core_ref, s_out,
    u_ref, diff_ref, vel_ref, coup_ref, bx_ref, by_ref, s_in,
    w, el, er, hl, hr, v, base, acc, th,
    a_ref, gyb, gzb, ct, ra, pbx, rb, pf, ry, pz, rp, pd, gh, gxb, ds, rd, pby, rdb, cot, rc, et, bxt, byt,
    s_halo, r_halo, s_yc, r_yc, s_zc, r_zc, s_py, r_py, s_pz, r_pz, s_zh, r_zh, s_px, r_px,
    s_ra, r_ra, s_rb, r_rb, s_rd, r_rd, s_rdb, r_rdb, s_co, r_co,
):
    sim = lax.axis_index("sim")
    zh = lax.axis_index("grp")
    x = lax.axis_index("gz")
    zl = sim // (2 * Q)
    y = (sim // 2) % Q
    c = sim % 2
    nsim = 2 * Q * Q
    nblk = Q * Q
    blk = zh * Q + x

    def dev(zl_, y_, c_, zh_, x_):
        return (zl_ * (2 * Q) + y_ * 2 + c_, zh_, x_)

    def cyc(i, d):
        return (i + d + Q) % Q

    def halo_dev(dx, dy):
        b = (blk + dy + nblk) % nblk
        return ((sim + dx + nsim) % nsim, b // Q, b % Q)

    pairs = [(d, e) for d in range(Q) for e in range(2) if (d, e) != (0, 0)]
    self_b = zl == zh
    self_d = x == y

    barrier = pltpu.get_barrier_semaphore()

    def tell(d):
        pl.semaphore_signal(barrier, inc=1, device_id=d, device_id_type=MESH)

    halo_dirs = [(dx, dy) for dx in (-1, 0, 1) for dy in (-1, 0, 1) if (dx, dy) != (0, 0)]
    for dx, dy in halo_dirs:
        tell(halo_dev(dx, dy))
    for d, e in pairs:
        tell(dev(zl, cyc(y, -d), c ^ e, zh, x))
        tell(dev(zl, y, c ^ e, zh, cyc(x, -d)))
        if d:
            tell(dev(cyc(zl, -d), y, c ^ e, zh, x))
    for d in range(1, Q):
        tell(dev(zl, y, c, cyc(zh, -d), x))
    for k in range(Q):
        @pl.when(~(self_b & (k == zh)))
        def _():
            tell(dev(zh, y, c, k, x))

        for e in range(2):
            @pl.when(~(self_d & (k == y) & (c == e)))
            def _():
                tell(dev(zl, k, e, zh, y))

    inputs = [
        pltpu.make_async_copy(src, dst, s_in.at[i])
        for i, (src, dst) in enumerate(
            [(u_hbm, u_ref), (diff_hbm, diff_ref), (vel_hbm, vel_ref), (coup_hbm, coup_ref), (bx_hbm, bx_ref), (by_hbm, by_ref)]
        )
    ]
    for copy in inputs:
        copy.start()

    sends = []

    def send(src, dst, ssem, rsem, target):
        copy = pltpu.make_async_remote_copy(
            src_ref=src, dst_ref=dst, send_sem=ssem, recv_sem=rsem, device_id=target, device_id_type=MESH
        )
        copy.start()
        sends.append(copy)

    def arrive(dst, ssem, rsem, source):
        pltpu.make_async_remote_copy(
            src_ref=dst, dst_ref=dst, send_sem=ssem, recv_sem=rsem, device_id=source, device_id_type=MESH
        ).wait_recv()

    def lane(shape):
        return lax.broadcasted_iota(jnp.int32, shape, len(shape) - 1)

    inputs[0].wait()
    zero = jnp.zeros((XR, LANES), F32)
    lane32 = lane((XR, LANES))
    left = zero
    right = zero
    for fz in range(NF * NZ):
        w[fz, 0:XR, :] = zero
        w[fz, 0:XR, 0:YC] = u_ref[fz // NZ, fz % NZ]
    for fz in range(NF * NZ):
        own = w[fz, 0:XR, :]
        here = lane32 // HALO == fz
        left = jnp.where(here, pltpu.roll(own, fz * HALO, 1) if fz else own, left)
        right = jnp.where(here, pltpu.roll(own, (fz * HALO - (YC - HALO)) % LANES, 1) if fz != 7 else own, right)
    el[...] = left
    er[...] = right

    out_count = jnp.int32(8 + 7 + 6 + 3 + 7 + 3 * Q) - self_b.astype(jnp.int32) - self_d.astype(jnp.int32)
    pl.semaphore_wait(barrier, out_count)

    def halo_sem(dx, dy):
        return (dx + 1) * 3 + dy + 1

    top, bottom = pl.ds(0, HALO), pl.ds(XR - HALO, HALO)
    below, above, mine = pl.ds(XR, HALO), pl.ds(XR + HALO, HALO), pl.ds(0, XR)
    halo_plan = [
        (-1, 0, w.at[:, top], w.at[:, below]),
        (1, 0, w.at[:, bottom], w.at[:, above]),
        (0, -1, el, hr.at[mine]),
        (0, 1, er, hl.at[mine]),
        (-1, -1, el.at[top], hr.at[below]),
        (1, -1, el.at[bottom], hr.at[above]),
        (-1, 1, er.at[top], hl.at[below]),
        (1, 1, er.at[bottom], hl.at[above]),
    ]
    for dx, dy, src, dst in halo_plan:
        i = halo_sem(dx, dy)
        send(src, dst, s_halo.at[i], r_halo.at[i], halo_dev(dx, dy))

    for copy in inputs[1:]:
        copy.wait()
    bxt[...] = bx_ref[pl.ds(pl.multiple_of((zl * Q + y) * 2 * XR, 2 * XR), 2 * XR), :].astype(F32).T.astype(BF16)
    byt[...] = jnp.concatenate(
        [
            by_ref[pl.ds(pl.multiple_of((k * Q + x) * YC + h * 32, 32), 32), :].astype(F32)
            for h in range(2) for k in range(Q)
        ],
        axis=0,
    ).T.astype(BF16)

    for dx, dy, src, dst in halo_plan:
        i = halo_sem(dx, dy)
        arrive(dst, s_halo.at[i], r_halo.at[i], halo_dev(-dx, -dy))

    lane48 = lane((ROWS, LANES))
    is_right = (lane48 >= YC) & (lane48 < YC + HALO)
    is_left = lane48 >= LANES - HALO
    for fz in range(NF * NZ):
        from_left = pltpu.roll(hl[...], (LANES - HALO - fz * HALO) % LANES, 1) if fz != 15 else hl[...]
        from_right = pltpu.roll(hr[...], (YC - fz * HALO) % LANES, 1) if fz != 8 else hr[...]
        full = jnp.where(is_left, from_left, jnp.where(is_right, from_right, w[fz]))
        v[fz // NZ, fz % NZ] = full
        base[fz // NZ, fz % NZ] = full
        th[0, fz // NZ, fz % NZ] = jnp.tanh(full)

    def step(_, carry):
        for stage in range(4):
            now, later = stage % 2, (stage + 1) % 2

            def field(f, carry2):
                d = diff_ref[f]
                vx = vel_ref[0, f] * 0.5
                vy = vel_ref[1, f] * 0.5
                for z in range(NZ):
                    s = v[f, z]
                    k = th[now, 0, z] * coup_ref[f, 0]
                    for g in range(1, NF):
                        k = k + th[now, g, z] * coup_ref[f, g]
                    k = k + s * (-6.0 * d) + pltpu.roll(s, ROWS - 1, 0) * (d - vx) + pltpu.roll(s, 1, 0) * (d + vx)
                    k = k + pltpu.roll(s, LANES - 1, 1) * (d - vy) + pltpu.roll(s, 1, 1) * (d + vy)
                    if z == 0:
                        first = k + v[f, 1] * (2.0 * d)
                        s0 = s
                    else:
                        second = k + s0 * (2.0 * d)
                for z, k in ((0, first), (1, second)):
                    if stage == 0:
                        acc[f, z] = k
                        new = base[f, z] + 0.5 * k
                    elif stage == 1:
                        acc[f, z] = acc[f, z] + 2.0 * k
                        new = base[f, z] + 0.5 * k
                    elif stage == 2:
                        acc[f, z] = acc[f, z] + 2.0 * k
                        new = base[f, z] + k
                    else:
                        new = base[f, z] + (acc[f, z] + k) * (1.0 / 6.0)
                        base[f, z] = new
                    v[f, z] = new
                    th[later, f, z] = jnp.tanh(new)
                return carry2

            lax.fori_loop(0, NF, field, 0)
        return carry

    lax.fori_loop(0, STEPS, step, 0)

    low32 = lane32 < YC
    for f in range(NF):
        a_ref[f] = jnp.where(low32, base[f, 0, 0:XR, :], pltpu.roll(base[f, 1, 0:XR, :], YC, 1))

    me_yc = y * 2 + c
    me_zc = c * Q + zl

    def send_rows_y(d, e):
        ty, tc = cyc(y, d), c ^ e
        send(a_ref.at[pl.ds(tc * HF, HF)], gyb.at[me_yc], s_yc.at[d * 2 + e], r_yc.at[me_yc], dev(zl, ty, tc, zh, x))

    def rows_y(d, e):
        sy, sc = cyc(y, -d), c ^ e
        i = sy * 2 + sc
        arrive(gyb.at[i], s_yc.at[d * 2 + e], r_yc.at[i], dev(zl, sy, sc, zh, x))

    send_rows_y(0, 1)
    for d, e in pairs:
        if d:
            tz, tc = cyc(zl, d), c ^ e
            send(a_ref.at[pl.ds(tc * HF, HF)], gzb.at[me_zc], s_zc.at[d * 2 + e], r_zc.at[me_zc], dev(tz, y, tc, zh, x))
    gyb[me_yc] = a_ref[pl.ds(c * HF, HF)]
    rows_y(0, 1)

    own = jnp.concatenate(
        [jnp.concatenate([gyb[y * 2, f], gyb[y * 2 + 1, f]], axis=0) for f in range(HF)], axis=1
    )
    oh, ol = split(own)
    part = dot(bxt[...], oh, NN) + dot(bxt[...], ol, NN)
    for k in range(Q):
        for j in range(Q):
            for f in range(HF):
                pf[k, j, f] = part[j * 32 + k * 8:j * 32 + k * 8 + 8, f * LANES:(f + 1) * LANES]
    for d in range(1, Q):
        ty = cyc(y, d)
        send(pf.at[ty], ry.at[y], s_py.at[d], r_py.at[y], dev(zl, ty, c, zh, x))
    for d, e in pairs:
        if d:
            send_rows_y(d, e)
    ry[y] = pf[y]
    for f in range(NF):
        for z in range(NZ):
            uo_ref[f, z] = base[f, z, 0:XR, 0:YC]
    outputs = [
        pltpu.make_async_copy(src, dst, s_out.at[i])
        for i, (src, dst) in enumerate([(uo_ref, uo_hbm), (gx_ref, gx_hbm), (gy_ref, gy_hbm), (core_ref, core_hbm)])
    ]
    outputs[0].start()
    for e in range(2):
        gzb[e * Q + zl] = gyb[y * 2 + e]
    for d in range(1, Q):
        sy = cyc(y, -d)
        arrive(ry.at[sy], s_py.at[d], r_py.at[sy], dev(zl, sy, c, zh, x))
    pz[...] = (ry[0] + ry[1]) + (ry[2] + ry[3])
    for d in range(1, Q):
        tz = cyc(zl, d)
        send(pz.at[tz], rp.at[zl], s_pz.at[d], r_pz.at[zl], dev(tz, y, c, zh, x))
    rp[zl] = pz[zl]
    for d in range(1, Q):
        sz = cyc(zl, -d)
        arrive(rp.at[sz], s_pz.at[d], r_pz.at[sz], dev(sz, y, c, zh, x))
    own = (rp[0] + rp[1]) + (rp[2] + rp[3])
    pd[...] = own
    for d in range(1, Q):
        th_ = cyc(zh, d)
        send(pd, gh.at[zh], s_zh.at[d], r_zh.at[zh], dev(zl, y, c, th_, x))
    for d in range(1, Q):
        tx = cyc(x, d)
        send(pd, gxb.at[x], s_px.at[d], r_px.at[x], dev(zl, y, c, zh, tx))
    gh[zh] = own
    gxb[x] = own

    def wide(ref):
        return jnp.concatenate([ref[:, f].reshape(2 * Q * XR, LANES) for f in range(HF)], axis=1)

    for d, e in pairs:
        if d:
            rows_y(d, e)
    gyh, gyl = split(wide(gyb))
    for d, e in pairs:
        if d:
            sz, sc = cyc(zl, -d), c ^ e
            i = sc * Q + sz
            arrive(gzb.at[i], s_zc.at[d * 2 + e], r_zc.at[i], dev(sz, y, sc, zh, x))
    gzh, gzl = split(wide(gzb))
    block = dot(gyh, gzh, NT) + (dot(gyh, gzl, NT) + dot(gyl, gzh, NT))
    for k in range(Q):
        for e in range(2):
            ct[k, e] = block[k * YC:(k + 1) * YC, e * LANES:(e + 1) * LANES]
    me_xc = x * 2 + c
    for d, e in pairs:
        tx, tc = cyc(x, d), c ^ e
        send(ct.at[tx, tc], ra.at[me_xc], s_ra.at[d * 2 + e], r_ra.at[me_xc], dev(zl, y, tc, zh, tx))
    ra[me_xc] = ct[x, c]

    for d, e in pairs:
        sx, sc = cyc(x, -d), c ^ e
        i = sx * 2 + sc
        arrive(ra.at[i], s_ra.at[d * 2 + e], r_ra.at[i], dev(zl, y, sc, zh, sx))
    low16 = lane((16, LANES)) < YC

    def fold(parts, out):
        total = parts[0]
        for i in range(1, 2 * Q):
            total = total + parts[i]
        turned = jnp.concatenate([total, total], axis=0).T
        for k in range(Q):
            out[k] = jnp.where(low16, turned[k * 32:k * 32 + 16], turned[k * 32 + 16:k * 32 + 32])

    def unfold(parts, out, scale):
        gsum = ((parts[0] + parts[1]) + (parts[2] + parts[3])) * scale
        out[0:16, :] = gsum[:, 0:YC]
        out[16:32, :] = pltpu.roll(gsum, YC, 1)[:, 0:YC]

    fold(ra, pbx)
    late = []
    for k in range(Q):
        same = self_b & (k == zl)
        copy = pltpu.make_async_remote_copy(
            src_ref=pbx.at[k], dst_ref=rb.at[zh], send_sem=s_rb.at[k], recv_sem=r_rb.at[zh],
            device_id=dev(k, y, c, zl, x), device_id_type=MESH,
        )
        late.append((same, copy))

        @pl.when(same)
        def _():
            rb[zh] = pbx[k]

        @pl.when(~same)
        def _():
            copy.start()

    for d in range(1, Q):
        sh = cyc(zh, -d)
        arrive(gh.at[sh], s_zh.at[d], r_zh.at[sh], dev(zl, y, c, sh, x))
    low = lane((32, LANES)) < YC

    def unpack(ref):
        g = [ref[k].reshape(32, LANES) for k in range(Q)]
        r = [pltpu.roll(t, YC, 1) for t in g]
        first = jnp.concatenate([jnp.where(low, g[0], r[1]), jnp.where(low, g[2], r[3])], axis=1)
        second = jnp.concatenate([jnp.where(low, r[0], g[1]), jnp.where(low, r[2], g[3])], axis=1)
        return jnp.concatenate([first, second], axis=0)

    def unpack_halves(ref):
        g = [ref[k].reshape(32, LANES) for k in range(Q)]
        quarter = lane((32, LANES)) // 32
        layers = []
        for z in range(NZ):
            halves = []
            for h in range(2):
                out = g[0]
                for k in range(Q):
                    shift = (k * 32 - z * 64 - h * 32) % LANES
                    moved = pltpu.roll(g[k], shift, 1) if shift else g[k]
                    out = moved if k == 0 else jnp.where(quarter == k, moved, out)
                halves.append(out)
            layers.append(jnp.concatenate(halves, axis=1))
        return jnp.concatenate(layers, axis=0)

    cols = unpack_halves(gh)
    ch, cl = split(cols)
    two_h = jnp.concatenate([ch, ch], axis=0)
    two_l = jnp.concatenate([cl, cl], axis=0)
    cot[...] = dot(byt[...], two_h, NT) + dot(byt[...], two_l, NT)

    def core_rows(x_):
        return pl.ds(pl.multiple_of(zh * 32 + x_ * 8, 8), 8)

    for d, e in pairs:
        tx, tc = cyc(x, d), c ^ e
        send(cot.at[core_rows(tx)], rc.at[me_xc], s_co.at[d * 2 + e], r_co.at[me_xc], dev(zl, y, tc, zh, tx))
    rc[me_xc] = cot[core_rows(x), :]

    for d in range(1, Q):
        sx = cyc(x, -d)
        arrive(gxb.at[sx], s_px.at[d], r_px.at[sx], dev(zl, y, c, zh, sx))
    rh, rl = split(unpack(gxb).T)
    dd = dot(rh, ch, NN) + (dot(rh, cl, NN) + dot(rl, ch, NN))
    for k in range(Q):
        for e in range(2):
            ds[k, e] = dd[k * YC:(k + 1) * YC, e * LANES:(e + 1) * LANES]
    for k in range(Q):
        for h in range(2):
            same = self_d & (k == x) & (c == h)
            copy = pltpu.make_async_remote_copy(
                src_ref=ds.at[k, h], dst_ref=rd.at[me_yc], send_sem=s_rd.at[k * 2 + h], recv_sem=r_rd.at[me_yc],
                device_id=dev(zl, x, h, zh, k), device_id_type=MESH,
            )
            late.append((same, copy))

            @pl.when(same)
            def _():
                rd[me_yc] = ds[k, h]

            @pl.when(~same)
            def _():
                copy.start()

    for k in range(Q):
        @pl.when(~(self_b & (k == zh)))
        def _():
            arrive(rb.at[k], s_rb.at[k], r_rb.at[k], dev(zh, y, c, k, x))
    unfold(rb, gx_ref, 1.0 / (NF * NZ * NY))
    outputs[1].start()

    for k in range(Q):
        for e in range(2):
            @pl.when(~(self_d & (k == y) & (c == e)))
            def _():
                arrive(rd.at[k * 2 + e], s_rd.at[k * 2 + e], r_rd.at[k * 2 + e], dev(zl, k, e, zh, y))
    fold(rd, pby)
    for d in range(1, Q):
        tz = cyc(zl, d)
        send(pby.at[tz], rdb.at[zl], s_rdb.at[d], r_rdb.at[zl], dev(tz, y, c, zh, x))
    rdb[zl] = pby[zl]

    for d, e in pairs:
        sx, sc = cyc(x, -d), c ^ e
        i = sx * 2 + sc
        arrive(rc.at[i], s_co.at[d * 2 + e], r_co.at[i], dev(zl, y, sc, zh, sx))
    e0 = (rc[0] + rc[2]) + (rc[4] + rc[6])
    e1 = (rc[1] + rc[3]) + (rc[5] + rc[7])
    both = jnp.where(lane((8, LANES)) < 64, e0, e1)
    et[...] = jnp.concatenate([both] * 16, axis=0).T
    for fh in range(2):
        for z in range(NZ):
            for f in range(HF):
                at = fh * 64 + z * 32 + f * 8
                core_ref[fh * HF + f, z] = jnp.where(c == 0, et[at:at + 4, 0:8], et[at + 4:at + 8, 0:8])

    outputs[3].start()

    for d in range(1, Q):
        sz = cyc(zl, -d)
        arrive(rdb.at[sz], s_rdb.at[d], r_rdb.at[sz], dev(sz, y, c, zh, x))
    unfold(rdb, gy_ref, 1.0 / (NF * NZ * RANK))
    outputs[2].start()

    for copy in outputs:
        copy.wait()
    for copy in sends:
        copy.wait_send()
    for same, copy in late:
        @pl.when(~same)
        def _():
            copy.wait_send()


def place(a, b, c, d, ao, bo, co, do, av, bv, cv, dv, sem):
    into = [pltpu.make_async_copy(src, dst, sem.at[i]) for i, (src, dst) in enumerate([(a, av), (b, bv), (c, cv), (d, dv)])]
    out = [
        pltpu.make_async_copy(src, dst, sem.at[4 + i]) for i, (src, dst) in enumerate([(av, ao), (bv, bo), (cv, co), (dv, do)])
    ]
    for copy in into:
        copy.start()
    for first, second in zip(into, out):
        first.wait()
        second.start()
    for copy in out:
        copy.wait()


def shards(fields, diffusivity, velocity, coupling, basis_x, basis_y):
    vm = lambda *shape: pltpu.VMEM(shape, F32)
    dma = lambda n: pltpu.SemaphoreType.DMA((n,))
    hspec = pl.BlockSpec(memory_space=pl.ANY)
    sm = lambda *shape: pltpu.SMEM(shape, F32)
    scratch = [
        vm(NF, NZ, XR, YC), vm(XR, YC), vm(XR, YC), vm(NF, NZ, 4, 8), dma(4),
        vm(NF, NZ, XR, YC), sm(NF), sm(2, NF), sm(NF, NF),
        pltpu.VMEM((NX, RANK), BF16), pltpu.VMEM((NY, RANK), BF16), dma(6),
        vm(NF * NZ, ROWS, LANES), vm(XR, LANES), vm(XR, LANES), vm(ROWS, LANES), vm(ROWS, LANES),
        vm(NF, NZ, ROWS, LANES), vm(NF, NZ, ROWS, LANES), vm(NF, NZ, ROWS, LANES), vm(2, NF, NZ, ROWS, LANES),
        vm(NF, XR, LANES),
        vm(2 * Q, HF, XR, LANES), vm(2 * Q, HF, XR, LANES),
        vm(Q, 2, YC, LANES), vm(2 * Q, YC, LANES), vm(Q, 16, LANES), vm(Q, 16, LANES),
        vm(Q, Q, HF, 8, LANES), vm(Q, Q, HF, 8, LANES), vm(Q, HF, 8, LANES),
        vm(Q, HF, 8, LANES), vm(HF, 8, LANES),
        vm(Q, HF, 8, LANES), vm(Q, HF, 8, LANES),
        vm(Q, 2, YC, LANES), vm(2 * Q, YC, LANES), vm(Q, 16, LANES), vm(Q, 16, LANES),
        vm(RANK, LANES), vm(2 * Q, 8, LANES), vm(LANES, LANES),
        pltpu.VMEM((RANK, 2 * XR), BF16), pltpu.VMEM((RANK, 256), BF16),
        dma(9), dma(9), dma(8), dma(8), dma(8), dma(8), dma(4), dma(4), dma(4), dma(4), dma(4), dma(4), dma(4), dma(4),
        dma(8), dma(8), dma(4), dma(4), dma(8), dma(8), dma(4), dma(4), dma(8), dma(8),
    ]
    shapes = (
        jax.ShapeDtypeStruct((NF, NZ, XR, YC), F32),
        jax.ShapeDtypeStruct((XR, YC), F32),
        jax.ShapeDtypeStruct((XR, YC), F32),
        jax.ShapeDtypeStruct((NF, NZ, 4, 8), F32),
    )
    parts = pl.pallas_call(
        kernel,
        out_shape=shapes,
        in_specs=[hspec] * 6,
        out_specs=(hspec,) * 4,
        scratch_shapes=scratch,
        compiler_params=pltpu.CompilerParams(
            collective_id=0, has_side_effects=True, vmem_limit_bytes=63 * 1024 * 1024
        ),
    )(fields, diffusivity, velocity, coupling, basis_x, basis_y)
    state, gram_x, gram_y, core = pl.pallas_call(
        place,
        out_shape=shapes,
        in_specs=[hspec] * 4,
        out_specs=(hspec,) * 4,
        scratch_shapes=[vm(NF, NZ, XR, YC), vm(XR, YC), vm(XR, YC), vm(NF, NZ, 4, 8), dma(8)],
        compiler_params=pltpu.CompilerParams(vmem_limit_bytes=63 * 1024 * 1024),
    )(*parts)
    return state, gram_x, gram_y.T, core


def solution(mesh):
    in_specs = (P(None, None, "sim", ("grp", "gz")), P(), P(), P(), P(), P())
    out_specs = (
        P(None, None, "sim", ("grp", "gz")),
        P("sim", ("grp", "gz")),
        P(("grp", "gz"), "sim"),
        P(None, None, "sim", ("grp", "gz")),
    )
    return jax.shard_map(shards, mesh=mesh, in_specs=in_specs, out_specs=out_specs, check_vma=False)
```

```python
import functools

import jax
import jax.numpy as jnp
from jax import lax
from jax.experimental import pallas as pl
from jax.experimental.pallas import tpu as pltpu
from jax.sharding import PartitionSpec as P

NF = 8
NX = 1024
NY = 1024
RANK = 128
NZ = 2
STEPS = 2
Q = 4
XR = 32
YC = 64
HALO = 8
ROWS = XR + 2 * HALO
LANES = 128
HF = NF // 2
MESH = pl.DeviceIdType.MESH
F32 = jnp.float32
BF16 = jnp.bfloat16


def split(a):
    hi = a.astype(BF16)
    lo = (a - hi.astype(F32)).astype(BF16)
    return hi, lo


def dot(a, b, dims):
    return lax.dot_general(a, b, (dims, ((), ())), preferred_element_type=F32)


def dot3(a, b, dims):
    ah, al = split(a)
    bh, bl = split(b)
    return dot(ah, bh, dims) + (dot(ah, bl, dims) + dot(al, bh, dims))


NN = ((1,), (0,))
NT = ((1,), (1,))


def kernel(
    u_hbm, diff_hbm, vel_hbm, coup_hbm, bx_hbm, by_hbm,
    uo_hbm, gx_hbm, gy_hbm, core_hbm,
    uo_ref, gx_ref, gy_ref, core_ref, s_out,
    u_ref, diff_ref, vel_ref, coup_ref, bx_ref, by_ref, s_in,
    w, el, er, hl, hr, v, base, acc, th,
    a_ref, gyb, gzb, ct, ra, pbx, rb, pf, ry, pz, rp, pd, gh, gxb, ds, rd, pby, rdb, cot, rc, et, bxt, byt,
    s_halo, r_halo, s_yc, r_yc, s_zc, r_zc, s_py, r_py, s_pz, r_pz, s_zh, r_zh, s_px, r_px,
    s_ra, r_ra, s_rb, r_rb, s_rd, r_rd, s_rdb, r_rdb, s_co, r_co,
):
    sim = lax.axis_index("sim")
    zh = lax.axis_index("grp")
    x = lax.axis_index("gz")
    zl = sim // (2 * Q)
    y = (sim // 2) % Q
    c = sim % 2
    nsim = 2 * Q * Q
    nblk = Q * Q
    blk = zh * Q + x

    def dev(zl_, y_, c_, zh_, x_):
        return (zl_ * (2 * Q) + y_ * 2 + c_, zh_, x_)

    def cyc(i, d):
        return (i + d + Q) % Q

    def halo_dev(dx, dy):
        b = (blk + dy + nblk) % nblk
        return ((sim + dx + nsim) % nsim, b // Q, b % Q)

    pairs = [(d, e) for d in range(Q) for e in range(2) if (d, e) != (0, 0)]
    self_b = zl == zh
    self_d = x == y

    barrier = pltpu.get_barrier_semaphore()

    def tell(d):
        pl.semaphore_signal(barrier, inc=1, device_id=d, device_id_type=MESH)

    halo_dirs = [(dx, dy) for dx in (-1, 0, 1) for dy in (-1, 0, 1) if (dx, dy) != (0, 0)]
    for dx, dy in halo_dirs:
        tell(halo_dev(dx, dy))
    for d, e in pairs:
        tell(dev(zl, cyc(y, -d), c ^ e, zh, x))
        tell(dev(zl, y, c ^ e, zh, cyc(x, -d)))
        if d:
            tell(dev(cyc(zl, -d), y, c ^ e, zh, x))
    for d in range(1, Q):
        tell(dev(zl, y, c, cyc(zh, -d), x))
    for k in range(Q):
        @pl.when(~(self_b & (k == zh)))
        def _():
            tell(dev(zh, y, c, k, x))

        for e in range(2):
            @pl.when(~(self_d & (k == y) & (c == e)))
            def _():
                tell(dev(zl, k, e, zh, y))

    inputs = [
        pltpu.make_async_copy(src, dst, s_in.at[i])
        for i, (src, dst) in enumerate(
            [(u_hbm, u_ref), (diff_hbm, diff_ref), (vel_hbm, vel_ref), (coup_hbm, coup_ref), (bx_hbm, bx_ref), (by_hbm, by_ref)]
        )
    ]
    for copy in inputs:
        copy.start()

    sends = []

    def send(src, dst, ssem, rsem, target):
        copy = pltpu.make_async_remote_copy(
            src_ref=src, dst_ref=dst, send_sem=ssem, recv_sem=rsem, device_id=target, device_id_type=MESH
        )
        copy.start()
        sends.append(copy)

    def arrive(dst, ssem, rsem, source):
        pltpu.make_async_remote_copy(
            src_ref=dst, dst_ref=dst, send_sem=ssem, recv_sem=rsem, device_id=source, device_id_type=MESH
        ).wait_recv()

    def lane(shape):
        return lax.broadcasted_iota(jnp.int32, shape, len(shape) - 1)

    inputs[0].wait()
    zero = jnp.zeros((XR, LANES), F32)
    lane32 = lane((XR, LANES))
    left = zero
    right = zero
    for fz in range(NF * NZ):
        w[fz, 0:XR, :] = zero
        w[fz, 0:XR, 0:YC] = u_ref[fz // NZ, fz % NZ]
    for fz in range(NF * NZ):
        own = w[fz, 0:XR, :]
        here = lane32 // HALO == fz
        left = jnp.where(here, pltpu.roll(own, fz * HALO, 1) if fz else own, left)
        right = jnp.where(here, pltpu.roll(own, (fz * HALO - (YC - HALO)) % LANES, 1) if fz != 7 else own, right)
    el[...] = left
    er[...] = right

    out_count = jnp.int32(8 + 7 + 6 + 3 + 7 + 3 * Q) - self_b.astype(jnp.int32) - self_d.astype(jnp.int32)
    pl.semaphore_wait(barrier, out_count)

    def halo_sem(dx, dy):
        return (dx + 1) * 3 + dy + 1

    top, bottom = pl.ds(0, HALO), pl.ds(XR - HALO, HALO)
    below, above, mine = pl.ds(XR, HALO), pl.ds(XR + HALO, HALO), pl.ds(0, XR)
    halo_plan = [
        (-1, 0, w.at[:, top], w.at[:, below]),
        (1, 0, w.at[:, bottom], w.at[:, above]),
        (0, -1, el, hr.at[mine]),
        (0, 1, er, hl.at[mine]),
        (-1, -1, el.at[top], hr.at[below]),
        (1, -1, el.at[bottom], hr.at[above]),
        (-1, 1, er.at[top], hl.at[below]),
        (1, 1, er.at[bottom], hl.at[above]),
    ]
    for dx, dy, src, dst in halo_plan:
        i = halo_sem(dx, dy)
        send(src, dst, s_halo.at[i], r_halo.at[i], halo_dev(dx, dy))

    for copy in inputs[1:]:
        copy.wait()
    bxt[...] = bx_ref[pl.ds(pl.multiple_of((zl * Q + y) * 2 * XR, 2 * XR), 2 * XR), :].astype(F32).T.astype(BF16)
    byt[...] = jnp.concatenate(
        [
            by_ref[pl.ds(pl.multiple_of((k * Q + x) * YC + h * 32, 32), 32), :].astype(F32)
            for h in range(2) for k in range(Q)
        ],
        axis=0,
    ).T.astype(BF16)

    for dx, dy, src, dst in halo_plan:
        i = halo_sem(dx, dy)
        arrive(dst, s_halo.at[i], r_halo.at[i], halo_dev(-dx, -dy))

    lane48 = lane((ROWS, LANES))
    is_right = (lane48 >= YC) & (lane48 < YC + HALO)
    is_left = lane48 >= LANES - HALO
    for fz in range(NF * NZ):
        from_left = pltpu.roll(hl[...], (LANES - HALO - fz * HALO) % LANES, 1) if fz != 15 else hl[...]
        from_right = pltpu.roll(hr[...], (YC - fz * HALO) % LANES, 1) if fz != 8 else hr[...]
        full = jnp.where(is_left, from_left, jnp.where(is_right, from_right, w[fz]))
        v[fz // NZ, fz % NZ] = full
        base[fz // NZ, fz % NZ] = full
        th[0, fz // NZ, fz % NZ] = jnp.tanh(full)

    def step(_, carry):
        for stage in range(4):
            now, later = stage % 2, (stage + 1) % 2

            for f in range(NF):
                d = diff_ref[f]
                vx = vel_ref[0, f] * 0.5
                vy = vel_ref[1, f] * 0.5
                for z in range(NZ):
                    s = v[f, z]
                    k = th[now, 0, z] * coup_ref[f, 0]
                    for g in range(1, NF):
                        k = k + th[now, g, z] * coup_ref[f, g]
                    k = k + s * (-6.0 * d) + pltpu.roll(s, ROWS - 1, 0) * (d - vx) + pltpu.roll(s, 1, 0) * (d + vx)
                    k = k + pltpu.roll(s, LANES - 1, 1) * (d - vy) + pltpu.roll(s, 1, 1) * (d + vy)
                    if z == 0:
                        first = k + v[f, 1] * (2.0 * d)
                        s0 = s
                    else:
                        second = k + s0 * (2.0 * d)
                for z, k in ((0, first), (1, second)):
                    if stage == 0:
                        acc[f, z] = k
                        new = base[f, z] + 0.5 * k
                    elif stage == 1:
                        acc[f, z] = acc[f, z] + 2.0 * k
                        new = base[f, z] + 0.5 * k
                    elif stage == 2:
                        acc[f, z] = acc[f, z] + 2.0 * k
                        new = base[f, z] + k
                    else:
                        new = base[f, z] + (acc[f, z] + k) * (1.0 / 6.0)
                        base[f, z] = new
                    v[f, z] = new
                    th[later, f, z] = jnp.tanh(new)
        return carry

    lax.fori_loop(0, STEPS, step, 0)

    low32 = lane32 < YC
    for f in range(NF):
        a_ref[f] = jnp.where(low32, base[f, 0, 0:XR, :], pltpu.roll(base[f, 1, 0:XR, :], YC, 1))

    me_yc = y * 2 + c
    me_zc = c * Q + zl

    def send_rows_y(d, e):
        ty, tc = cyc(y, d), c ^ e
        send(a_ref.at[pl.ds(tc * HF, HF)], gyb.at[me_yc], s_yc.at[d * 2 + e], r_yc.at[me_yc], dev(zl, ty, tc, zh, x))

    def rows_y(d, e):
        sy, sc = cyc(y, -d), c ^ e
        i = sy * 2 + sc
        arrive(gyb.at[i], s_yc.at[d * 2 + e], r_yc.at[i], dev(zl, sy, sc, zh, x))

    send_rows_y(0, 1)
    for d, e in pairs:
        if d:
            tz, tc = cyc(zl, d), c ^ e
            send(a_ref.at[pl.ds(tc * HF, HF)], gzb.at[me_zc], s_zc.at[d * 2 + e], r_zc.at[me_zc], dev(tz, y, tc, zh, x))
    gyb[me_yc] = a_ref[pl.ds(c * HF, HF)]
    rows_y(0, 1)

    own = jnp.concatenate(
        [jnp.concatenate([gyb[y * 2, f], gyb[y * 2 + 1, f]], axis=0) for f in range(HF)], axis=1
    )
    oh, ol = split(own)
    part = dot(bxt[...], oh, NN) + dot(bxt[...], ol, NN)
    for k in range(Q):
        for j in range(Q):
            for f in range(HF):
                pf[k, j, f] = part[j * 32 + k * 8:j * 32 + k * 8 + 8, f * LANES:(f + 1) * LANES]
    for d in range(1, Q):
        ty = cyc(y, d)
        send(pf.at[ty], ry.at[y], s_py.at[d], r_py.at[y], dev(zl, ty, c, zh, x))
    for d, e in pairs:
        if d:
            send_rows_y(d, e)
    ry[y] = pf[y]
    for f in range(NF):
        for z in range(NZ):
            uo_ref[f, z] = base[f, z, 0:XR, 0:YC]
    outputs = [
        pltpu.make_async_copy(src, dst, s_out.at[i])
        for i, (src, dst) in enumerate([(uo_ref, uo_hbm), (gx_ref, gx_hbm), (gy_ref, gy_hbm), (core_ref, core_hbm)])
    ]
    outputs[0].start()
    for e in range(2):
        gzb[e * Q + zl] = gyb[y * 2 + e]
    for d in range(1, Q):
        sy = cyc(y, -d)
        arrive(ry.at[sy], s_py.at[d], r_py.at[sy], dev(zl, sy, c, zh, x))
    pz[...] = (ry[0] + ry[1]) + (ry[2] + ry[3])
    for d in range(1, Q):
        tz = cyc(zl, d)
        send(pz.at[tz], rp.at[zl], s_pz.at[d], r_pz.at[zl], dev(tz, y, c, zh, x))
    rp[zl] = pz[zl]
    for d in range(1, Q):
        sz = cyc(zl, -d)
        arrive(rp.at[sz], s_pz.at[d], r_pz.at[sz], dev(sz, y, c, zh, x))
    own = (rp[0] + rp[1]) + (rp[2] + rp[3])
    pd[...] = own
    for d in range(1, Q):
        th_ = cyc(zh, d)
        send(pd, gh.at[zh], s_zh.at[d], r_zh.at[zh], dev(zl, y, c, th_, x))
    for d in range(1, Q):
        tx = cyc(x, d)
        send(pd, gxb.at[x], s_px.at[d], r_px.at[x], dev(zl, y, c, zh, tx))
    gh[zh] = own
    gxb[x] = own

    def wide(ref):
        return jnp.concatenate([ref[:, f].reshape(2 * Q * XR, LANES) for f in range(HF)], axis=1)

    for d, e in pairs:
        if d:
            rows_y(d, e)
    gyh, gyl = split(wide(gyb))
    for d, e in pairs:
        if d:
            sz, sc = cyc(zl, -d), c ^ e
            i = sc * Q + sz
            arrive(gzb.at[i], s_zc.at[d * 2 + e], r_zc.at[i], dev(sz, y, sc, zh, x))
    gzh, gzl = split(wide(gzb))
    block = dot(gyh, gzh, NT) + (dot(gyh, gzl, NT) + dot(gyl, gzh, NT))
    for k in range(Q):
        for e in range(2):
            ct[k, e] = block[k * YC:(k + 1) * YC, e * LANES:(e + 1) * LANES]
    me_xc = x * 2 + c
    for d, e in pairs:
        tx, tc = cyc(x, d), c ^ e
        send(ct.at[tx, tc], ra.at[me_xc], s_ra.at[d * 2 + e], r_ra.at[me_xc], dev(zl, y, tc, zh, tx))
    ra[me_xc] = ct[x, c]

    for d, e in pairs:
        sx, sc = cyc(x, -d), c ^ e
        i = sx * 2 + sc
        arrive(ra.at[i], s_ra.at[d * 2 + e], r_ra.at[i], dev(zl, y, sc, zh, sx))
    low16 = lane((16, LANES)) < YC

    def fold(parts, out):
        total = parts[0]
        for i in range(1, 2 * Q):
            total = total + parts[i]
        turned = jnp.concatenate([total, total], axis=0).T
        for k in range(Q):
            out[k] = jnp.where(low16, turned[k * 32:k * 32 + 16], turned[k * 32 + 16:k * 32 + 32])

    def unfold(parts, out, scale):
        gsum = ((parts[0] + parts[1]) + (parts[2] + parts[3])) * scale
        out[0:16, :] = gsum[:, 0:YC]
        out[16:32, :] = pltpu.roll(gsum, YC, 1)[:, 0:YC]

    fold(ra, pbx)
    late = []
    for k in range(Q):
        same = self_b & (k == zl)
        copy = pltpu.make_async_remote_copy(
            src_ref=pbx.at[k], dst_ref=rb.at[zh], send_sem=s_rb.at[k], recv_sem=r_rb.at[zh],
            device_id=dev(k, y, c, zl, x), device_id_type=MESH,
        )
        late.append((same, copy))

        @pl.when(same)
        def _():
            rb[zh] = pbx[k]

        @pl.when(~same)
        def _():
            copy.start()

    for d in range(1, Q):
        sh = cyc(zh, -d)
        arrive(gh.at[sh], s_zh.at[d], r_zh.at[sh], dev(zl, y, c, sh, x))
    low = lane((32, LANES)) < YC

    def unpack(ref):
        g = [ref[k].reshape(32, LANES) for k in range(Q)]
        r = [pltpu.roll(t, YC, 1) for t in g]
        first = jnp.concatenate([jnp.where(low, g[0], r[1]), jnp.where(low, g[2], r[3])], axis=1)
        second = jnp.concatenate([jnp.where(low, r[0], g[1]), jnp.where(low, r[2], g[3])], axis=1)
        return jnp.concatenate([first, second], axis=0)

    def unpack_halves(ref):
        g = [ref[k].reshape(32, LANES) for k in range(Q)]
        quarter = lane((32, LANES)) // 32
        layers = []
        for z in range(NZ):
            halves = []
            for h in range(2):
                out = g[0]
                for k in range(Q):
                    shift = (k * 32 - z * 64 - h * 32) % LANES
                    moved = pltpu.roll(g[k], shift, 1) if shift else g[k]
                    out = moved if k == 0 else jnp.where(quarter == k, moved, out)
                halves.append(out)
            layers.append(jnp.concatenate(halves, axis=1))
        return jnp.concatenate(layers, axis=0)

    cols = unpack_halves(gh)
    ch, cl = split(cols)
    two_h = jnp.concatenate([ch, ch], axis=0)
    two_l = jnp.concatenate([cl, cl], axis=0)
    cot[...] = dot(byt[...], two_h, NT) + dot(byt[...], two_l, NT)

    def core_rows(x_):
        return pl.ds(pl.multiple_of(zh * 32 + x_ * 8, 8), 8)

    for d, e in pairs:
        tx, tc = cyc(x, d), c ^ e
        send(cot.at[core_rows(tx)], rc.at[me_xc], s_co.at[d * 2 + e], r_co.at[me_xc], dev(zl, y, tc, zh, tx))
    rc[me_xc] = cot[core_rows(x), :]

    for d in range(1, Q):
        sx = cyc(x, -d)
        arrive(gxb.at[sx], s_px.at[d], r_px.at[sx], dev(zl, y, c, zh, sx))
    rh, rl = split(unpack(gxb).T)
    dd = dot(rh, ch, NN) + (dot(rh, cl, NN) + dot(rl, ch, NN))
    for k in range(Q):
        for e in range(2):
            ds[k, e] = dd[k * YC:(k + 1) * YC, e * LANES:(e + 1) * LANES]
    for k in range(Q):
        for h in range(2):
            same = self_d & (k == x) & (c == h)
            copy = pltpu.make_async_remote_copy(
                src_ref=ds.at[k, h], dst_ref=rd.at[me_yc], send_sem=s_rd.at[k * 2 + h], recv_sem=r_rd.at[me_yc],
                device_id=dev(zl, x, h, zh, k), device_id_type=MESH,
            )
            late.append((same, copy))

            @pl.when(same)
            def _():
                rd[me_yc] = ds[k, h]

            @pl.when(~same)
            def _():
                copy.start()

    for k in range(Q):
        @pl.when(~(self_b & (k == zh)))
        def _():
            arrive(rb.at[k], s_rb.at[k], r_rb.at[k], dev(zh, y, c, k, x))
    unfold(rb, gx_ref, 1.0 / (NF * NZ * NY))
    outputs[1].start()

    for k in range(Q):
        for e in range(2):
            @pl.when(~(self_d & (k == y) & (c == e)))
            def _():
                arrive(rd.at[k * 2 + e], s_rd.at[k * 2 + e], r_rd.at[k * 2 + e], dev(zl, k, e, zh, y))
    fold(rd, pby)
    for d in range(1, Q):
        tz = cyc(zl, d)
        send(pby.at[tz], rdb.at[zl], s_rdb.at[d], r_rdb.at[zl], dev(tz, y, c, zh, x))
    rdb[zl] = pby[zl]

    for d, e in pairs:
        sx, sc = cyc(x, -d), c ^ e
        i = sx * 2 + sc
        arrive(rc.at[i], s_co.at[d * 2 + e], r_co.at[i], dev(zl, y, sc, zh, sx))
    e0 = (rc[0] + rc[2]) + (rc[4] + rc[6])
    e1 = (rc[1] + rc[3]) + (rc[5] + rc[7])
    both = jnp.where(lane((8, LANES)) < 64, e0, e1)
    et[...] = jnp.concatenate([both] * 16, axis=0).T
    for fh in range(2):
        for z in range(NZ):
            for f in range(HF):
                at = fh * 64 + z * 32 + f * 8
                core_ref[fh * HF + f, z] = jnp.where(c == 0, et[at:at + 4, 0:8], et[at + 4:at + 8, 0:8])

    outputs[3].start()

    for d in range(1, Q):
        sz = cyc(zl, -d)
        arrive(rdb.at[sz], s_rdb.at[d], r_rdb.at[sz], dev(sz, y, c, zh, x))
    unfold(rdb, gy_ref, 1.0 / (NF * NZ * RANK))
    outputs[2].start()

    for copy in outputs:
        copy.wait()
    for copy in sends:
        copy.wait_send()
    for same, copy in late:
        @pl.when(~same)
        def _():
            copy.wait_send()


def place(a, b, c, d, ao, bo, co, do, av, bv, cv, dv, sem):
    into = [pltpu.make_async_copy(src, dst, sem.at[i]) for i, (src, dst) in enumerate([(a, av), (b, bv), (c, cv), (d, dv)])]
    out = [
        pltpu.make_async_copy(src, dst, sem.at[4 + i]) for i, (src, dst) in enumerate([(av, ao), (bv, bo), (cv, co), (dv, do)])
    ]
    for copy in into:
        copy.start()
    for first, second in zip(into, out):
        first.wait()
        second.start()
    for copy in out:
        copy.wait()


def shards(fields, diffusivity, velocity, coupling, basis_x, basis_y):
    vm = lambda *shape: pltpu.VMEM(shape, F32)
    dma = lambda n: pltpu.SemaphoreType.DMA((n,))
    hspec = pl.BlockSpec(memory_space=pl.ANY)
    sm = lambda *shape: pltpu.SMEM(shape, F32)
    scratch = [
        vm(NF, NZ, XR, YC), vm(XR, YC), vm(XR, YC), vm(NF, NZ, 4, 8), dma(4),
        vm(NF, NZ, XR, YC), sm(NF), sm(2, NF), sm(NF, NF),
        pltpu.VMEM((NX, RANK), BF16), pltpu.VMEM((NY, RANK), BF16), dma(6),
        vm(NF * NZ, ROWS, LANES), vm(XR, LANES), vm(XR, LANES), vm(ROWS, LANES), vm(ROWS, LANES),
        vm(NF, NZ, ROWS, LANES), vm(NF, NZ, ROWS, LANES), vm(NF, NZ, ROWS, LANES), vm(2, NF, NZ, ROWS, LANES),
        vm(NF, XR, LANES),
        vm(2 * Q, HF, XR, LANES), vm(2 * Q, HF, XR, LANES),
        vm(Q, 2, YC, LANES), vm(2 * Q, YC, LANES), vm(Q, 16, LANES), vm(Q, 16, LANES),
        vm(Q, Q, HF, 8, LANES), vm(Q, Q, HF, 8, LANES), vm(Q, HF, 8, LANES),
        vm(Q, HF, 8, LANES), vm(HF, 8, LANES),
        vm(Q, HF, 8, LANES), vm(Q, HF, 8, LANES),
        vm(Q, 2, YC, LANES), vm(2 * Q, YC, LANES), vm(Q, 16, LANES), vm(Q, 16, LANES),
        vm(RANK, LANES), vm(2 * Q, 8, LANES), vm(LANES, LANES),
        pltpu.VMEM((RANK, 2 * XR), BF16), pltpu.VMEM((RANK, 256), BF16),
        dma(9), dma(9), dma(8), dma(8), dma(8), dma(8), dma(4), dma(4), dma(4), dma(4), dma(4), dma(4), dma(4), dma(4),
        dma(8), dma(8), dma(4), dma(4), dma(8), dma(8), dma(4), dma(4), dma(8), dma(8),
    ]
    shapes = (
        jax.ShapeDtypeStruct((NF, NZ, XR, YC), F32),
        jax.ShapeDtypeStruct((XR, YC), F32),
        jax.ShapeDtypeStruct((XR, YC), F32),
        jax.ShapeDtypeStruct((NF, NZ, 4, 8), F32),
    )
    parts = pl.pallas_call(
        kernel,
        out_shape=shapes,
        in_specs=[hspec] * 6,
        out_specs=(hspec,) * 4,
        scratch_shapes=scratch,
        compiler_params=pltpu.CompilerParams(
            collective_id=0, has_side_effects=True, vmem_limit_bytes=63 * 1024 * 1024
        ),
    )(fields, diffusivity, velocity, coupling, basis_x, basis_y)
    state, gram_x, gram_y, core = pl.pallas_call(
        place,
        out_shape=shapes,
        in_specs=[hspec] * 4,
        out_specs=(hspec,) * 4,
        scratch_shapes=[vm(NF, NZ, XR, YC), vm(XR, YC), vm(XR, YC), vm(NF, NZ, 4, 8), dma(8)],
        compiler_params=pltpu.CompilerParams(vmem_limit_bytes=63 * 1024 * 1024),
    )(*parts)
    return state, gram_x, gram_y.T, core


def solution(mesh):
    in_specs = (P(None, None, "sim", ("grp", "gz")), P(), P(), P(), P(), P())
    out_specs = (
        P(None, None, "sim", ("grp", "gz")),
        P("sim", ("grp", "gz")),
        P(("grp", "gz"), "sim"),
        P(None, None, "sim", ("grp", "gz")),
    )
    return jax.shard_map(shards, mesh=mesh, in_specs=in_specs, out_specs=out_specs, check_vma=False)
```

```python
import functools

import jax
import jax.numpy as jnp
from jax import lax
from jax.experimental import pallas as pl
from jax.experimental.pallas import tpu as pltpu
from jax.sharding import PartitionSpec as P

NF = 8
NX = 1024
NY = 1024
RANK = 128
NZ = 2
STEPS = 2
Q = 4
XR = 32
YC = 64
HALO = 8
ROWS = XR + 2 * HALO
LANES = 128
HF = NF // 2
MESH = pl.DeviceIdType.MESH
F32 = jnp.float32
BF16 = jnp.bfloat16


def split(a):
    hi = a.astype(BF16)
    lo = (a - hi.astype(F32)).astype(BF16)
    return hi, lo


def dot(a, b, dims):
    return lax.dot_general(a, b, (dims, ((), ())), preferred_element_type=F32)


def dot3(a, b, dims):
    ah, al = split(a)
    bh, bl = split(b)
    return dot(ah, bh, dims) + (dot(ah, bl, dims) + dot(al, bh, dims))


NN = ((1,), (0,))
NT = ((1,), (1,))


def kernel(
    u_hbm, diff_hbm, vel_hbm, coup_hbm, bx_hbm, by_hbm,
    uo_hbm, gx_hbm, gy_hbm, core_hbm,
    uo_ref, gx_ref, gy_ref, core_ref, s_out,
    u_ref, diff_ref, vel_ref, coup_ref, bx_ref, by_ref, s_in,
    w, el, er, hl, hr, v, base, acc, th,
    a_ref, gyb, gzb, ct, ra, pbx, rb, pf, ry, pz, rp, pd, gh, gxb, gh2, gx2, ds, rd, pby, rdb, cot, rc, et, bxt, byt,
    s_halo, r_halo, s_yc, r_yc, s_zc, r_zc, s_py, r_py, s_pz, r_pz, s_zh, r_zh, s_px, r_px, s_fh, r_fh, s_fx, r_fx,
    s_ra, r_ra, s_rb, r_rb, s_rd, r_rd, s_rdb, r_rdb, s_co, r_co,
):
    sim = lax.axis_index("sim")
    zh = lax.axis_index("grp")
    x = lax.axis_index("gz")
    zl = sim // (2 * Q)
    y = (sim // 2) % Q
    c = sim % 2
    nsim = 2 * Q * Q
    nblk = Q * Q
    blk = zh * Q + x

    def dev(zl_, y_, c_, zh_, x_):
        return (zl_ * (2 * Q) + y_ * 2 + c_, zh_, x_)

    def cyc(i, d):
        return (i + d + Q) % Q

    def halo_dev(dx, dy):
        b = (blk + dy + nblk) % nblk
        return ((sim + dx + nsim) % nsim, b // Q, b % Q)

    pairs = [(d, e) for d in range(Q) for e in range(2) if (d, e) != (0, 0)]
    self_b = zl == zh
    self_d = x == y

    barrier = pltpu.get_barrier_semaphore()

    def tell(d):
        pl.semaphore_signal(barrier, inc=1, device_id=d, device_id_type=MESH)

    halo_dirs = [(dx, dy) for dx in (-1, 0, 1) for dy in (-1, 0, 1) if (dx, dy) != (0, 0)]
    for dx, dy in halo_dirs:
        tell(halo_dev(dx, dy))
    inputs = [
        pltpu.make_async_copy(src, dst, s_in.at[i])
        for i, (src, dst) in enumerate(
            [(u_hbm, u_ref), (diff_hbm, diff_ref), (vel_hbm, vel_ref), (coup_hbm, coup_ref), (bx_hbm, bx_ref), (by_hbm, by_ref)]
        )
    ]
    for copy in inputs:
        copy.start()
    for d, e in pairs:
        tell(dev(zl, cyc(y, -d), c ^ e, zh, x))
        tell(dev(zl, y, c ^ e, zh, cyc(x, -d)))
        if d:
            tell(dev(cyc(zl, -d), y, c ^ e, zh, x))
    for d in range(1, Q):
        tell(dev(zl, y, c, cyc(zh, -d), x))
    for k in range(Q):
        @pl.when(~(self_b & (k == zh)))
        def _():
            tell(dev(zh, y, c, k, x))

        @pl.when(~(self_d & (k == y)))
        def _():
            tell(dev(zl, k, c, zh, y))

    sends = []

    def send(src, dst, ssem, rsem, target):
        copy = pltpu.make_async_remote_copy(
            src_ref=src, dst_ref=dst, send_sem=ssem, recv_sem=rsem, device_id=target, device_id_type=MESH
        )
        copy.start()
        sends.append(copy)

    def arrive(dst, ssem, rsem, source):
        pltpu.make_async_remote_copy(
            src_ref=dst, dst_ref=dst, send_sem=ssem, recv_sem=rsem, device_id=source, device_id_type=MESH
        ).wait_recv()

    def lane(shape):
        return lax.broadcasted_iota(jnp.int32, shape, len(shape) - 1)

    inputs[0].wait()
    zero = jnp.zeros((XR, LANES), F32)
    lane32 = lane((XR, LANES))
    left = zero
    right = zero
    for fz in range(NF * NZ):
        w[fz, 0:XR, :] = zero
        w[fz, 0:XR, 0:YC] = u_ref[fz // NZ, fz % NZ]
    for fz in range(NF * NZ):
        own = w[fz, 0:XR, :]
        here = lane32 // HALO == fz
        left = jnp.where(here, pltpu.roll(own, fz * HALO, 1) if fz else own, left)
        right = jnp.where(here, pltpu.roll(own, (fz * HALO - (YC - HALO)) % LANES, 1) if fz != 7 else own, right)
    el[...] = left
    er[...] = right

    out_count = jnp.int32(8 + 7 + 6 + 3 + 7 + 2 * Q) - self_b.astype(jnp.int32) - self_d.astype(jnp.int32)
    pl.semaphore_wait(barrier, out_count)

    def halo_sem(dx, dy):
        return (dx + 1) * 3 + dy + 1

    top, bottom = pl.ds(0, HALO), pl.ds(XR - HALO, HALO)
    below, above, mine = pl.ds(XR, HALO), pl.ds(XR + HALO, HALO), pl.ds(0, XR)
    halo_plan = [
        (-1, 0, w.at[:, top], w.at[:, below]),
        (1, 0, w.at[:, bottom], w.at[:, above]),
        (0, -1, el, hr.at[mine]),
        (0, 1, er, hl.at[mine]),
        (-1, -1, el.at[top], hr.at[below]),
        (1, -1, el.at[bottom], hr.at[above]),
        (-1, 1, er.at[top], hl.at[below]),
        (1, 1, er.at[bottom], hl.at[above]),
    ]
    for dx, dy, src, dst in halo_plan:
        i = halo_sem(dx, dy)
        send(src, dst, s_halo.at[i], r_halo.at[i], halo_dev(dx, dy))

    for copy in inputs[1:]:
        copy.wait()
    bxt[...] = bx_ref[pl.ds(pl.multiple_of((zl * Q + y) * 2 * XR, 2 * XR), 2 * XR), :].astype(F32).T.astype(BF16)
    byt[...] = jnp.concatenate(
        [
            by_ref[pl.ds(pl.multiple_of((k * Q + x) * YC + h * 32, 32), 32), :].astype(F32)
            for h in range(2) for k in range(Q)
        ],
        axis=0,
    ).T.astype(BF16)

    for dx, dy, src, dst in halo_plan:
        i = halo_sem(dx, dy)
        arrive(dst, s_halo.at[i], r_halo.at[i], halo_dev(-dx, -dy))

    lane48 = lane((ROWS, LANES))
    is_right = (lane48 >= YC) & (lane48 < YC + HALO)
    is_left = lane48 >= LANES - HALO
    for fz in range(NF * NZ):
        from_left = pltpu.roll(hl[...], (LANES - HALO - fz * HALO) % LANES, 1) if fz != 15 else hl[...]
        from_right = pltpu.roll(hr[...], (YC - fz * HALO) % LANES, 1) if fz != 8 else hr[...]
        full = jnp.where(is_left, from_left, jnp.where(is_right, from_right, w[fz]))
        v[fz // NZ, fz % NZ] = full
        base[fz // NZ, fz % NZ] = full
        th[0, fz // NZ, fz % NZ] = jnp.tanh(full)

    def step(_, carry):
        for stage in range(4):
            now, later = stage % 2, (stage + 1) % 2

            for f in range(NF):
                d = diff_ref[f]
                vx = vel_ref[0, f] * 0.5
                vy = vel_ref[1, f] * 0.5
                for z in range(NZ):
                    s = v[f, z]
                    k = th[now, 0, z] * coup_ref[f, 0]
                    for g in range(1, NF):
                        k = k + th[now, g, z] * coup_ref[f, g]
                    k = k + s * (-6.0 * d) + pltpu.roll(s, ROWS - 1, 0) * (d - vx) + pltpu.roll(s, 1, 0) * (d + vx)
                    k = k + pltpu.roll(s, LANES - 1, 1) * (d - vy) + pltpu.roll(s, 1, 1) * (d + vy)
                    if z == 0:
                        first = k + v[f, 1] * (2.0 * d)
                        s0 = s
                    else:
                        second = k + s0 * (2.0 * d)
                for z, k in ((0, first), (1, second)):
                    if stage == 0:
                        acc[f, z] = k
                        new = base[f, z] + 0.5 * k
                    elif stage == 1:
                        acc[f, z] = acc[f, z] + 2.0 * k
                        new = base[f, z] + 0.5 * k
                    elif stage == 2:
                        acc[f, z] = acc[f, z] + 2.0 * k
                        new = base[f, z] + k
                    else:
                        new = base[f, z] + (acc[f, z] + k) * (1.0 / 6.0)
                        base[f, z] = new
                    v[f, z] = new
                    th[later, f, z] = jnp.tanh(new)
        return carry

    lax.fori_loop(0, STEPS, step, 0)

    low32 = lane32 < YC
    for f in range(NF):
        a_ref[f] = jnp.where(low32, base[f, 0, 0:XR, :], pltpu.roll(base[f, 1, 0:XR, :], YC, 1))

    me_yc = y * 2 + c
    me_zc = c * Q + zl

    def send_rows_y(d, e):
        ty, tc = cyc(y, d), c ^ e
        send(a_ref.at[pl.ds(tc * HF, HF)], gyb.at[me_yc], s_yc.at[d * 2 + e], r_yc.at[me_yc], dev(zl, ty, tc, zh, x))

    def rows_y(d, e):
        sy, sc = cyc(y, -d), c ^ e
        i = sy * 2 + sc
        arrive(gyb.at[i], s_yc.at[d * 2 + e], r_yc.at[i], dev(zl, sy, sc, zh, x))

    send_rows_y(0, 1)
    for d, e in pairs:
        if d:
            tz, tc = cyc(zl, d), c ^ e
            send(a_ref.at[pl.ds(tc * HF, HF)], gzb.at[me_zc], s_zc.at[d * 2 + e], r_zc.at[me_zc], dev(tz, y, tc, zh, x))
    gyb[me_yc] = a_ref[pl.ds(c * HF, HF)]
    rows_y(0, 1)

    own = jnp.concatenate(
        [jnp.concatenate([gyb[y * 2, f], gyb[y * 2 + 1, f]], axis=0) for f in range(HF)], axis=1
    )
    oh, ol = split(own)
    part = dot(bxt[...], oh, NN) + dot(bxt[...], ol, NN)
    for k in range(Q):
        for j in range(Q):
            for f in range(HF):
                pf[k, j, f] = part[j * 32 + k * 8:j * 32 + k * 8 + 8, f * LANES:(f + 1) * LANES]
    for d in range(1, Q):
        ty = cyc(y, d)
        send(pf.at[ty], ry.at[y], s_py.at[d], r_py.at[y], dev(zl, ty, c, zh, x))
    for d, e in pairs:
        if d:
            send_rows_y(d, e)
    ry[y] = pf[y]
    for f in range(NF):
        for z in range(NZ):
            uo_ref[f, z] = base[f, z, 0:XR, 0:YC]
    outputs = [
        pltpu.make_async_copy(src, dst, s_out.at[i])
        for i, (src, dst) in enumerate([(uo_ref, uo_hbm), (gx_ref, gx_hbm), (gy_ref, gy_hbm), (core_ref, core_hbm)])
    ]
    outputs[0].start()
    for e in range(2):
        gzb[e * Q + zl] = gyb[y * 2 + e]
    for d in range(1, Q):
        sy = cyc(y, -d)
        arrive(ry.at[sy], s_py.at[d], r_py.at[sy], dev(zl, sy, c, zh, x))
    pz[...] = (ry[0] + ry[1]) + (ry[2] + ry[3])
    for d in range(1, Q):
        tz = cyc(zl, d)
        send(pz.at[tz], rp.at[zl], s_pz.at[d], r_pz.at[zl], dev(tz, y, c, zh, x))
    rp[zl] = pz[zl]
    for d in range(1, Q):
        sz = cyc(zl, -d)
        arrive(rp.at[sz], s_pz.at[d], r_pz.at[sz], dev(sz, y, c, zh, x))
    own = (rp[0] + rp[1]) + (rp[2] + rp[3])
    pd[...] = own
    for d in range(1, Q):
        th_ = cyc(zh, d)
        send(pd, gh.at[zh], s_zh.at[d], r_zh.at[zh], dev(zl, y, c, th_, x))
    for d in range(1, Q):
        tx = cyc(x, d)
        send(pd, gxb.at[x], s_px.at[d], r_px.at[x], dev(zl, y, c, zh, tx))
    sibling = dev(zl, y, c ^ 1, zh, x)
    send(pd, gx2.at[x], s_fx.at[0], r_fx.at[x], sibling)
    send(pd, gh2.at[zh], s_fh.at[0], r_fh.at[zh], sibling)
    gh[zh] = own
    gxb[x] = own

    def wide(ref):
        return jnp.concatenate([ref[:, f].reshape(2 * Q * XR, LANES) for f in range(HF)], axis=1)

    for d, e in pairs:
        if d:
            rows_y(d, e)
    gyh, gyl = split(wide(gyb))
    for d, e in pairs:
        if d:
            sz, sc = cyc(zl, -d), c ^ e
            i = sc * Q + sz
            arrive(gzb.at[i], s_zc.at[d * 2 + e], r_zc.at[i], dev(sz, y, sc, zh, x))
    gzh, gzl = split(wide(gzb))
    block = dot(gyh, gzh, NT) + (dot(gyh, gzl, NT) + dot(gyl, gzh, NT))
    for k in range(Q):
        for e in range(2):
            ct[k, e] = block[k * YC:(k + 1) * YC, e * LANES:(e + 1) * LANES]
    me_xc = x * 2 + c
    for d, e in pairs:
        tx, tc = cyc(x, d), c ^ e
        send(ct.at[tx, tc], ra.at[me_xc], s_ra.at[d * 2 + e], r_ra.at[me_xc], dev(zl, y, tc, zh, tx))
    ra[me_xc] = ct[x, c]

    late = []
    low = lane((32, LANES)) < YC

    def unpack(ref):
        g = [ref[k].reshape(32, LANES) for k in range(Q)]
        r = [pltpu.roll(t, YC, 1) for t in g]
        first = jnp.concatenate([jnp.where(low, g[0], r[1]), jnp.where(low, g[2], r[3])], axis=1)
        second = jnp.concatenate([jnp.where(low, r[0], g[1]), jnp.where(low, r[2], g[3])], axis=1)
        return jnp.concatenate([first, second], axis=0)

    quarter = lane((32, LANES)) // 32

    def pack_half(g, h):
        layers = []
        for z in range(NZ):
            out = g[0]
            for k in range(Q):
                shift = (k * 32 - z * 64 - h * 32) % LANES
                moved = pltpu.roll(g[k], shift, 1) if shift else g[k]
                out = moved if k == 0 else jnp.where(quarter == k, moved, out)
            layers.append(out)
        return jnp.concatenate(layers, axis=0)

    for d in range(1, Q):
        sx = cyc(x, -d)
        arrive(gxb.at[sx], s_px.at[d], r_px.at[sx], dev(zl, y, c, zh, sx))
        send(gxb.at[sx], gx2.at[sx], s_fx.at[d], r_fx.at[sx], sibling)
    for k in range(Q):
        arrive(gx2.at[k], s_fx.at[k], r_fx.at[k], sibling)
    rh, rl = split(jnp.concatenate([unpack(gxb), unpack(gx2)], axis=0).T)

    for d in (1, 3, 2):
        sh = cyc(zh, -d)
        arrive(gh.at[sh], s_zh.at[d], r_zh.at[sh], dev(zl, y, c, sh, x))
        send(gh.at[sh], gh2.at[sh], s_fh.at[d], r_fh.at[sh], sibling)
    mine_g = [gh[k].reshape(32, LANES) for k in range(Q)]
    halves = [pack_half(mine_g, h) for h in range(2)]
    for k in range(Q):
        arrive(gh2.at[k], s_fh.at[k], r_fh.at[k], sibling)
    other_g = [gh2[k].reshape(32, LANES) for k in range(Q)]
    other_g = [jnp.where(c == 0, t, pltpu.roll(t, LANES - 32, 1)) for t in other_g]
    kcols = jnp.concatenate([jnp.where(c == 0, halves[0], halves[1]), pack_half(other_g, 0)], axis=0)
    kh, kl = split(kcols)
    dd = dot(rh, kh, NN) + (dot(rh, kl, NN) + dot(rl, kh, NN))
    for k in range(Q):
        ds[k] = dd[k * YC:(k + 1) * YC]
    for k in range(Q):
        same = self_d & (k == x)
        copy = pltpu.make_async_remote_copy(
            src_ref=ds.at[k], dst_ref=rd.at[y], send_sem=s_rd.at[k], recv_sem=r_rd.at[y],
            device_id=dev(zl, x, c, zh, k), device_id_type=MESH,
        )
        late.append((same, copy))

        @pl.when(same)
        def _():
            rd[y] = ds[k]

        @pl.when(~same)
        def _():
            copy.start()

    ch, cl = split(jnp.concatenate(halves, axis=1))
    two_h = jnp.concatenate([ch, ch], axis=0)
    two_l = jnp.concatenate([cl, cl], axis=0)
    cot[...] = dot(byt[...], two_h, NT) + dot(byt[...], two_l, NT)

    def core_rows(x_):
        return pl.ds(pl.multiple_of(zh * 32 + x_ * 8, 8), 8)

    for d, e in pairs:
        tx, tc = cyc(x, d), c ^ e
        send(cot.at[core_rows(tx)], rc.at[me_xc], s_co.at[d * 2 + e], r_co.at[me_xc], dev(zl, y, tc, zh, tx))
    rc[me_xc] = cot[core_rows(x), :]

    for d, e in pairs:
        sx, sc = cyc(x, -d), c ^ e
        i = sx * 2 + sc
        arrive(ra.at[i], s_ra.at[d * 2 + e], r_ra.at[i], dev(zl, y, sc, zh, sx))
    low16 = lane((16, LANES)) < YC

    def fold(parts, out, count):
        total = parts[0]
        for i in range(1, count):
            total = total + parts[i]
        turned = jnp.concatenate([total, total], axis=0).T
        for k in range(Q):
            out[k] = jnp.where(low16, turned[k * 32:k * 32 + 16], turned[k * 32 + 16:k * 32 + 32])

    def unfold(parts, out, scale):
        gsum = ((parts[0] + parts[1]) + (parts[2] + parts[3])) * scale
        out[0:16, :] = gsum[:, 0:YC]
        out[16:32, :] = pltpu.roll(gsum, YC, 1)[:, 0:YC]

    fold(ra, pbx, 2 * Q)
    for k in range(Q):
        same = self_b & (k == zl)
        copy = pltpu.make_async_remote_copy(
            src_ref=pbx.at[k], dst_ref=rb.at[zh], send_sem=s_rb.at[k], recv_sem=r_rb.at[zh],
            device_id=dev(k, y, c, zl, x), device_id_type=MESH,
        )
        late.append((same, copy))

        @pl.when(same)
        def _():
            rb[zh] = pbx[k]

        @pl.when(~same)
        def _():
            copy.start()

    for k in range(Q):
        @pl.when(~(self_d & (k == y)))
        def _():
            arrive(rd.at[k], s_rd.at[k], r_rd.at[k], dev(zl, k, c, zh, y))
    fold(rd, pby, Q)
    for d in range(1, Q):
        tz = cyc(zl, d)
        send(pby.at[tz], rdb.at[zl], s_rdb.at[d], r_rdb.at[zl], dev(tz, y, c, zh, x))
    rdb[zl] = pby[zl]

    for d, e in pairs:
        sx, sc = cyc(x, -d), c ^ e
        i = sx * 2 + sc
        arrive(rc.at[i], s_co.at[d * 2 + e], r_co.at[i], dev(zl, y, sc, zh, sx))
    e0 = (rc[0] + rc[2]) + (rc[4] + rc[6])
    e1 = (rc[1] + rc[3]) + (rc[5] + rc[7])
    both = jnp.where(lane((8, LANES)) < 64, e0, e1)
    et[...] = jnp.concatenate([both] * 16, axis=0).T
    for fh in range(2):
        for z in range(NZ):
            for f in range(HF):
                at = fh * 64 + z * 32 + f * 8
                core_ref[fh * HF + f, z] = jnp.where(c == 0, et[at:at + 4, 0:8], et[at + 4:at + 8, 0:8])

    outputs[3].start()

    for k in range(Q):
        @pl.when(~(self_b & (k == zh)))
        def _():
            arrive(rb.at[k], s_rb.at[k], r_rb.at[k], dev(zh, y, c, k, x))
    unfold(rb, gx_ref, 1.0 / (NF * NZ * NY))
    outputs[1].start()

    for d in range(1, Q):
        sz = cyc(zl, -d)
        arrive(rdb.at[sz], s_rdb.at[d], r_rdb.at[sz], dev(sz, y, c, zh, x))
    unfold(rdb, gy_ref, 1.0 / (NF * NZ * RANK))
    outputs[2].start()

    for copy in outputs:
        copy.wait()
    for copy in sends:
        copy.wait_send()
    for same, copy in late:
        @pl.when(~same)
        def _():
            copy.wait_send()


def place(a, b, c, d, ao, bo, co, do, av, bv, cv, dv, sem):
    into = [pltpu.make_async_copy(src, dst, sem.at[i]) for i, (src, dst) in enumerate([(a, av), (b, bv), (c, cv), (d, dv)])]
    out = [
        pltpu.make_async_copy(src, dst, sem.at[4 + i]) for i, (src, dst) in enumerate([(av, ao), (bv, bo), (cv, co), (dv, do)])
    ]
    for copy in into:
        copy.start()
    for first, second in zip(into, out):
        first.wait()
        second.start()
    for copy in out:
        copy.wait()


def shards(fields, diffusivity, velocity, coupling, basis_x, basis_y):
    vm = lambda *shape: pltpu.VMEM(shape, F32)
    dma = lambda n: pltpu.SemaphoreType.DMA((n,))
    hspec = pl.BlockSpec(memory_space=pl.ANY)
    sm = lambda *shape: pltpu.SMEM(shape, F32)
    scratch = [
        vm(NF, NZ, XR, YC), vm(XR, YC), vm(XR, YC), vm(NF, NZ, 4, 8), dma(4),
        vm(NF, NZ, XR, YC), sm(NF), sm(2, NF), sm(NF, NF),
        pltpu.VMEM((NX, RANK), BF16), pltpu.VMEM((NY, RANK), BF16), dma(6),
        vm(NF * NZ, ROWS, LANES), vm(XR, LANES), vm(XR, LANES), vm(ROWS, LANES), vm(ROWS, LANES),
        vm(NF, NZ, ROWS, LANES), vm(NF, NZ, ROWS, LANES), vm(NF, NZ, ROWS, LANES), vm(2, NF, NZ, ROWS, LANES),
        vm(NF, XR, LANES),
        vm(2 * Q, HF, XR, LANES), vm(2 * Q, HF, XR, LANES),
        vm(Q, 2, YC, LANES), vm(2 * Q, YC, LANES), vm(Q, 16, LANES), vm(Q, 16, LANES),
        vm(Q, Q, HF, 8, LANES), vm(Q, Q, HF, 8, LANES), vm(Q, HF, 8, LANES),
        vm(Q, HF, 8, LANES), vm(HF, 8, LANES),
        vm(Q, HF, 8, LANES), vm(Q, HF, 8, LANES), vm(Q, HF, 8, LANES), vm(Q, HF, 8, LANES),
        vm(Q, YC, LANES), vm(Q, YC, LANES), vm(Q, 16, LANES), vm(Q, 16, LANES),
        vm(RANK, LANES), vm(2 * Q, 8, LANES), vm(LANES, LANES),
        pltpu.VMEM((RANK, 2 * XR), BF16), pltpu.VMEM((RANK, 256), BF16),
        dma(9), dma(9), dma(8), dma(8), dma(8), dma(8), dma(4), dma(4), dma(4), dma(4), dma(4), dma(4), dma(4), dma(4), dma(4), dma(4), dma(4), dma(4),
        dma(8), dma(8), dma(4), dma(4), dma(4), dma(4), dma(4), dma(4), dma(8), dma(8),
    ]
    shapes = (
        jax.ShapeDtypeStruct((NF, NZ, XR, YC), F32),
        jax.ShapeDtypeStruct((XR, YC), F32),
        jax.ShapeDtypeStruct((XR, YC), F32),
        jax.ShapeDtypeStruct((NF, NZ, 4, 8), F32),
    )
    parts = pl.pallas_call(
        kernel,
        out_shape=shapes,
        in_specs=[hspec] * 6,
        out_specs=(hspec,) * 4,
        scratch_shapes=scratch,
        compiler_params=pltpu.CompilerParams(
            collective_id=0, has_side_effects=True, vmem_limit_bytes=63 * 1024 * 1024
        ),
    )(fields, diffusivity, velocity, coupling, basis_x, basis_y)
    state, gram_x, gram_y, core = pl.pallas_call(
        place,
        out_shape=shapes,
        in_specs=[hspec] * 4,
        out_specs=(hspec,) * 4,
        scratch_shapes=[vm(NF, NZ, XR, YC), vm(XR, YC), vm(XR, YC), vm(NF, NZ, 4, 8), dma(8)],
        compiler_params=pltpu.CompilerParams(vmem_limit_bytes=63 * 1024 * 1024),
    )(*parts)
    return state, gram_x, gram_y.T, core


def solution(mesh):
    in_specs = (P(None, None, "sim", ("grp", "gz")), P(), P(), P(), P(), P())
    out_specs = (
        P(None, None, "sim", ("grp", "gz")),
        P("sim", ("grp", "gz")),
        P(("grp", "gz"), "sim"),
        P(None, None, "sim", ("grp", "gz")),
    )
    return jax.shard_map(shards, mesh=mesh, in_specs=in_specs, out_specs=out_specs, check_vma=False)
```

```python
import functools

import jax
import jax.numpy as jnp
from jax import lax
from jax.experimental import pallas as pl
from jax.experimental.pallas import tpu as pltpu
from jax.sharding import PartitionSpec as P

NF = 8
NX = 1024
NY = 1024
RANK = 128
NZ = 2
STEPS = 2
Q = 4
XR = 32
YC = 64
HALO = 8
ROWS = XR + 2 * HALO
LANES = 128
HF = NF // 2
MESH = pl.DeviceIdType.MESH
F32 = jnp.float32
BF16 = jnp.bfloat16


def split(a):
    hi = a.astype(BF16)
    lo = (a - hi.astype(F32)).astype(BF16)
    return hi, lo


def dot(a, b, dims):
    return lax.dot_general(a, b, (dims, ((), ())), preferred_element_type=F32)


def dot3(a, b, dims):
    ah, al = split(a)
    bh, bl = split(b)
    return dot(ah, bh, dims) + (dot(ah, bl, dims) + dot(al, bh, dims))


NN = ((1,), (0,))
NT = ((1,), (1,))


def kernel(
    u_hbm, diff_hbm, vel_hbm, coup_hbm, bx_hbm, by_hbm,
    uo_hbm, gx_hbm, gy_hbm, core_hbm,
    uo_ref, gx_ref, gy_ref, core_ref, s_out,
    u_ref, diff_ref, vel_ref, coup_ref, bx_ref, by_ref, s_in,
    w, el, er, hl, hr, v, base, acc, th,
    a_ref, gyb, gzb, ct, ra, pbx, rb, pf, ry, pz, rp, pd, gh, gxb, gh2, gx2, ds, rd, pby, rdb, cot, rc, et, bxt, byt,
    s_halo, r_halo, s_yc, r_yc, s_zc, r_zc, s_py, r_py, s_pz, r_pz, s_zh, r_zh, s_px, r_px, s_fh, r_fh, s_fx, r_fx,
    s_ra, r_ra, s_rb, r_rb, s_rd, r_rd, s_rdb, r_rdb, s_co, r_co,
):
    sim = lax.axis_index("sim")
    zh = lax.axis_index("grp")
    x = lax.axis_index("gz")
    zl = sim // (2 * Q)
    y = (sim // 2) % Q
    c = sim % 2
    nsim = 2 * Q * Q
    nblk = Q * Q
    blk = zh * Q + x

    def dev(zl_, y_, c_, zh_, x_):
        return (zl_ * (2 * Q) + y_ * 2 + c_, zh_, x_)

    def cyc(i, d):
        return (i + d + Q) % Q

    def halo_dev(dx, dy):
        b = (blk + dy + nblk) % nblk
        return ((sim + dx + nsim) % nsim, b // Q, b % Q)

    pairs = [(d, e) for d in range(Q) for e in range(2) if (d, e) != (0, 0)]
    self_b = zl == zh
    self_d = x == y

    barrier = pltpu.get_barrier_semaphore()

    def tell(d):
        pl.semaphore_signal(barrier, inc=1, device_id=d, device_id_type=MESH)

    halo_dirs = [(dx, dy) for dx in (-1, 0, 1) for dy in (-1, 0, 1) if (dx, dy) != (0, 0)]
    for dx, dy in halo_dirs:
        tell(halo_dev(dx, dy))
    inputs = [
        pltpu.make_async_copy(src, dst, s_in.at[i])
        for i, (src, dst) in enumerate(
            [(u_hbm, u_ref), (diff_hbm, diff_ref), (vel_hbm, vel_ref), (coup_hbm, coup_ref), (bx_hbm, bx_ref), (by_hbm, by_ref)]
        )
    ]
    for copy in inputs:
        copy.start()
    for d, e in pairs:
        tell(dev(zl, cyc(y, -d), c ^ e, zh, x))
        tell(dev(zl, y, c ^ e, zh, cyc(x, -d)))
        if d:
            tell(dev(cyc(zl, -d), y, c ^ e, zh, x))
    for d in range(1, Q):
        tell(dev(zl, y, c, cyc(zh, -d), x))
    for k in range(Q):
        @pl.when(~(self_b & (k == zh)))
        def _():
            tell(dev(zh, y, c, k, x))

        @pl.when(~(self_d & (k == y)))
        def _():
            tell(dev(zl, k, c, zh, y))

    sends = []

    def send(src, dst, ssem, rsem, target):
        copy = pltpu.make_async_remote_copy(
            src_ref=src, dst_ref=dst, send_sem=ssem, recv_sem=rsem, device_id=target, device_id_type=MESH
        )
        copy.start()
        sends.append(copy)

    def arrive(dst, ssem, rsem, source):
        pltpu.make_async_remote_copy(
            src_ref=dst, dst_ref=dst, send_sem=ssem, recv_sem=rsem, device_id=source, device_id_type=MESH
        ).wait_recv()

    def lane(shape):
        return lax.broadcasted_iota(jnp.int32, shape, len(shape) - 1)

    inputs[0].wait()
    zero = jnp.zeros((XR, LANES), F32)
    lane32 = lane((XR, LANES))
    left = zero
    right = zero
    for fz in range(NF * NZ):
        w[fz, 0:XR, :] = zero
        w[fz, 0:XR, 0:YC] = u_ref[fz // NZ, fz % NZ]
    for fz in range(NF * NZ):
        own = w[fz, 0:XR, :]
        here = lane32 // HALO == fz
        left = jnp.where(here, pltpu.roll(own, fz * HALO, 1) if fz else own, left)
        right = jnp.where(here, pltpu.roll(own, (fz * HALO - (YC - HALO)) % LANES, 1) if fz != 7 else own, right)
    el[...] = left
    er[...] = right

    out_count = jnp.int32(8 + 7 + 6 + 3 + 7 + 2 * Q) - self_b.astype(jnp.int32) - self_d.astype(jnp.int32)
    pl.semaphore_wait(barrier, out_count)

    def halo_sem(dx, dy):
        return (dx + 1) * 3 + dy + 1

    top, bottom = pl.ds(0, HALO), pl.ds(XR - HALO, HALO)
    below, above, mine = pl.ds(XR, HALO), pl.ds(XR + HALO, HALO), pl.ds(0, XR)
    halo_plan = [
        (-1, 0, w.at[:, top], w.at[:, below]),
        (1, 0, w.at[:, bottom], w.at[:, above]),
        (0, -1, el, hr.at[mine]),
        (0, 1, er, hl.at[mine]),
        (-1, -1, el.at[top], hr.at[below]),
        (1, -1, el.at[bottom], hr.at[above]),
        (-1, 1, er.at[top], hl.at[below]),
        (1, 1, er.at[bottom], hl.at[above]),
    ]
    for dx, dy, src, dst in halo_plan:
        i = halo_sem(dx, dy)
        send(src, dst, s_halo.at[i], r_halo.at[i], halo_dev(dx, dy))

    for copy in inputs[1:]:
        copy.wait()
    bxt[...] = bx_ref[pl.ds(pl.multiple_of((zl * Q + y) * 2 * XR, 2 * XR), 2 * XR), :].astype(F32).T.astype(BF16)
    byt[...] = jnp.concatenate(
        [
            by_ref[pl.ds(pl.multiple_of((k * Q + x) * YC + h * 32, 32), 32), :].astype(F32)
            for h in range(2) for k in range(Q)
        ],
        axis=0,
    ).T.astype(BF16)

    for dx, dy, src, dst in halo_plan:
        i = halo_sem(dx, dy)
        arrive(dst, s_halo.at[i], r_halo.at[i], halo_dev(-dx, -dy))

    lane48 = lane((ROWS, LANES))
    is_right = (lane48 >= YC) & (lane48 < YC + HALO)
    is_left = lane48 >= LANES - HALO
    for fz in range(NF * NZ):
        from_left = pltpu.roll(hl[...], (LANES - HALO - fz * HALO) % LANES, 1) if fz != 15 else hl[...]
        from_right = pltpu.roll(hr[...], (YC - fz * HALO) % LANES, 1) if fz != 8 else hr[...]
        full = jnp.where(is_left, from_left, jnp.where(is_right, from_right, w[fz]))
        v[fz // NZ, fz % NZ] = full
        base[fz // NZ, fz % NZ] = full
        th[0, fz // NZ, fz % NZ] = jnp.tanh(full)

    def step(_, carry):
        for stage in range(4):
            now, later = stage % 2, (stage + 1) % 2

            for f in range(NF):
                d = diff_ref[f]
                vx = vel_ref[0, f] * 0.5
                vy = vel_ref[1, f] * 0.5
                for z in range(NZ):
                    s = v[f, z]
                    k = th[now, 0, z] * coup_ref[f, 0]
                    for g in range(1, NF):
                        k = k + th[now, g, z] * coup_ref[f, g]
                    k = k + s * (-6.0 * d) + pltpu.roll(s, ROWS - 1, 0) * (d - vx) + pltpu.roll(s, 1, 0) * (d + vx)
                    k = k + pltpu.roll(s, LANES - 1, 1) * (d - vy) + pltpu.roll(s, 1, 1) * (d + vy)
                    if z == 0:
                        first = k + v[f, 1] * (2.0 * d)
                        s0 = s
                    else:
                        second = k + s0 * (2.0 * d)
                for z, k in ((0, first), (1, second)):
                    if stage == 0:
                        acc[f, z] = k
                        new = base[f, z] + 0.5 * k
                    elif stage == 1:
                        acc[f, z] = acc[f, z] + 2.0 * k
                        new = base[f, z] + 0.5 * k
                    elif stage == 2:
                        acc[f, z] = acc[f, z] + 2.0 * k
                        new = base[f, z] + k
                    else:
                        new = base[f, z] + (acc[f, z] + k) * (1.0 / 6.0)
                        base[f, z] = new
                    v[f, z] = new
                    th[later, f, z] = jnp.tanh(new)
        return carry

    lax.fori_loop(0, STEPS, step, 0)

    low32 = lane32 < YC
    for f in range(NF):
        a_ref[f] = jnp.where(low32, base[f, 0, 0:XR, :], pltpu.roll(base[f, 1, 0:XR, :], YC, 1))

    me_yc = y * 2 + c
    me_zc = c * Q + zl

    def send_rows_y(d, e):
        ty, tc = cyc(y, d), c ^ e
        send(a_ref.at[pl.ds(tc * HF, HF)], gyb.at[me_yc], s_yc.at[d * 2 + e], r_yc.at[me_yc], dev(zl, ty, tc, zh, x))

    def rows_y(d, e):
        sy, sc = cyc(y, -d), c ^ e
        i = sy * 2 + sc
        arrive(gyb.at[i], s_yc.at[d * 2 + e], r_yc.at[i], dev(zl, sy, sc, zh, x))

    send_rows_y(0, 1)
    for d, e in pairs:
        if d:
            tz, tc = cyc(zl, d), c ^ e
            send(a_ref.at[pl.ds(tc * HF, HF)], gzb.at[me_zc], s_zc.at[d * 2 + e], r_zc.at[me_zc], dev(tz, y, tc, zh, x))
    gyb[me_yc] = a_ref[pl.ds(c * HF, HF)]
    rows_y(0, 1)

    own = jnp.concatenate(
        [jnp.concatenate([gyb[y * 2, f], gyb[y * 2 + 1, f]], axis=0) for f in range(HF)], axis=1
    )
    oh, ol = split(own)
    part = dot(bxt[...], oh, NN) + dot(bxt[...], ol, NN)
    for k in range(Q):
        for j in range(Q):
            for f in range(HF):
                pf[k, j, f] = part[j * 32 + k * 8:j * 32 + k * 8 + 8, f * LANES:(f + 1) * LANES]
    for d in range(1, Q):
        ty = cyc(y, d)
        send(pf.at[ty], ry.at[y], s_py.at[d], r_py.at[y], dev(zl, ty, c, zh, x))
    for d, e in pairs:
        if d:
            send_rows_y(d, e)
    ry[y] = pf[y]
    for f in range(NF):
        for z in range(NZ):
            uo_ref[f, z] = base[f, z, 0:XR, 0:YC]
    outputs = [
        pltpu.make_async_copy(src, dst, s_out.at[i])
        for i, (src, dst) in enumerate([(uo_ref, uo_hbm), (gx_ref, gx_hbm), (gy_ref, gy_hbm), (core_ref, core_hbm)])
    ]
    outputs[0].start()
    for e in range(2):
        gzb[e * Q + zl] = gyb[y * 2 + e]
    for d in range(1, Q):
        sy = cyc(y, -d)
        arrive(ry.at[sy], s_py.at[d], r_py.at[sy], dev(zl, sy, c, zh, x))
    pz[...] = (ry[0] + ry[1]) + (ry[2] + ry[3])
    for d in range(1, Q):
        tz = cyc(zl, d)
        send(pz.at[tz], rp.at[zl], s_pz.at[d], r_pz.at[zl], dev(tz, y, c, zh, x))
    rp[zl] = pz[zl]
    for d in range(1, Q):
        sz = cyc(zl, -d)
        arrive(rp.at[sz], s_pz.at[d], r_pz.at[sz], dev(sz, y, c, zh, x))
    own = (rp[0] + rp[1]) + (rp[2] + rp[3])
    pd[...] = own
    for d in range(1, Q):
        th_ = cyc(zh, d)
        send(pd, gh.at[zh], s_zh.at[d], r_zh.at[zh], dev(zl, y, c, th_, x))
    for d in range(1, Q):
        tx = cyc(x, d)
        send(pd, gxb.at[x], s_px.at[d], r_px.at[x], dev(zl, y, c, zh, tx))
    sibling = dev(zl, y, c ^ 1, zh, x)
    send(pd, gx2.at[x], s_fx.at[0], r_fx.at[x], sibling)
    send(pd, gh2.at[zh], s_fh.at[0], r_fh.at[zh], sibling)
    gh[zh] = own
    gxb[x] = own

    def wide(ref):
        return jnp.concatenate([ref[:, f].reshape(2 * Q * XR, LANES) for f in range(HF)], axis=1)

    for d, e in pairs:
        if d:
            rows_y(d, e)
    gyh, gyl = split(wide(gyb))
    for d, e in pairs:
        if d:
            sz, sc = cyc(zl, -d), c ^ e
            i = sc * Q + sz
            arrive(gzb.at[i], s_zc.at[d * 2 + e], r_zc.at[i], dev(sz, y, sc, zh, x))
    gzh, gzl = split(wide(gzb))
    block = dot(gyh, gzh, NT) + (dot(gyh, gzl, NT) + dot(gyl, gzh, NT))
    for k in range(Q):
        for e in range(2):
            ct[k, e] = block[k * YC:(k + 1) * YC, e * LANES:(e + 1) * LANES]
    me_xc = x * 2 + c
    for d, e in pairs:
        tx, tc = cyc(x, d), c ^ e
        send(ct.at[tx, tc], ra.at[me_xc], s_ra.at[d * 2 + e], r_ra.at[me_xc], dev(zl, y, tc, zh, tx))
    ra[me_xc] = ct[x, c]

    late = []
    low = lane((32, LANES)) < YC

    def unpack(ref):
        g = [ref[k].reshape(32, LANES) for k in range(Q)]
        r = [pltpu.roll(t, YC, 1) for t in g]
        first = jnp.concatenate([jnp.where(low, g[0], r[1]), jnp.where(low, g[2], r[3])], axis=1)
        second = jnp.concatenate([jnp.where(low, r[0], g[1]), jnp.where(low, r[2], g[3])], axis=1)
        return jnp.concatenate([first, second], axis=0)

    quarter = lane((32, LANES)) // 32

    def pack_half(g, h):
        layers = []
        for z in range(NZ):
            out = g[0]
            for k in range(Q):
                shift = (k * 32 - z * 64 - h * 32) % LANES
                moved = pltpu.roll(g[k], shift, 1) if shift else g[k]
                out = moved if k == 0 else jnp.where(quarter == k, moved, out)
            layers.append(out)
        return jnp.concatenate(layers, axis=0)

    for d in range(1, Q):
        sx = cyc(x, -d)
        arrive(gxb.at[sx], s_px.at[d], r_px.at[sx], dev(zl, y, c, zh, sx))
        send(gxb.at[sx], gx2.at[sx], s_fx.at[d], r_fx.at[sx], sibling)
    for k in range(Q):
        arrive(gx2.at[k], s_fx.at[k], r_fx.at[k], sibling)
    rh, rl = split(jnp.concatenate([unpack(gxb), unpack(gx2)], axis=0).T)

    for d, e in pairs:
        sx, sc = cyc(x, -d), c ^ e
        i = sx * 2 + sc
        arrive(ra.at[i], s_ra.at[d * 2 + e], r_ra.at[i], dev(zl, y, sc, zh, sx))
    low16 = lane((16, LANES)) < YC

    def fold(parts, out, count):
        total = parts[0]
        for i in range(1, count):
            total = total + parts[i]
        turned = jnp.concatenate([total, total], axis=0).T
        for k in range(Q):
            out[k] = jnp.where(low16, turned[k * 32:k * 32 + 16], turned[k * 32 + 16:k * 32 + 32])

    def unfold(parts, out, scale):
        gsum = ((parts[0] + parts[1]) + (parts[2] + parts[3])) * scale
        out[0:16, :] = gsum[:, 0:YC]
        out[16:32, :] = pltpu.roll(gsum, YC, 1)[:, 0:YC]

    fold(ra, pbx, 2 * Q)
    for k in range(Q):
        same = self_b & (k == zl)
        copy = pltpu.make_async_remote_copy(
            src_ref=pbx.at[k], dst_ref=rb.at[zh], send_sem=s_rb.at[k], recv_sem=r_rb.at[zh],
            device_id=dev(k, y, c, zl, x), device_id_type=MESH,
        )
        late.append((same, copy))

        @pl.when(same)
        def _():
            rb[zh] = pbx[k]

        @pl.when(~same)
        def _():
            copy.start()

    for d in (1, 3, 2):
        sh = cyc(zh, -d)
        arrive(gh.at[sh], s_zh.at[d], r_zh.at[sh], dev(zl, y, c, sh, x))
        send(gh.at[sh], gh2.at[sh], s_fh.at[d], r_fh.at[sh], sibling)
    mine_g = [gh[k].reshape(32, LANES) for k in range(Q)]
    halves = [pack_half(mine_g, h) for h in range(2)]
    for k in range(Q):
        arrive(gh2.at[k], s_fh.at[k], r_fh.at[k], sibling)
    other_g = [gh2[k].reshape(32, LANES) for k in range(Q)]
    other_g = [jnp.where(c == 0, t, pltpu.roll(t, LANES - 32, 1)) for t in other_g]
    kcols = jnp.concatenate([jnp.where(c == 0, halves[0], halves[1]), pack_half(other_g, 0)], axis=0)
    kh, kl = split(kcols)
    dd = dot(rh, kh, NN) + (dot(rh, kl, NN) + dot(rl, kh, NN))
    for k in range(Q):
        ds[k] = dd[k * YC:(k + 1) * YC]
    for k in range(Q):
        same = self_d & (k == x)
        copy = pltpu.make_async_remote_copy(
            src_ref=ds.at[k], dst_ref=rd.at[y], send_sem=s_rd.at[k], recv_sem=r_rd.at[y],
            device_id=dev(zl, x, c, zh, k), device_id_type=MESH,
        )
        late.append((same, copy))

        @pl.when(same)
        def _():
            rd[y] = ds[k]

        @pl.when(~same)
        def _():
            copy.start()

    ch, cl = split(jnp.concatenate(halves, axis=1))
    two_h = jnp.concatenate([ch, ch], axis=0)
    two_l = jnp.concatenate([cl, cl], axis=0)
    cot[...] = dot(byt[...], two_h, NT) + dot(byt[...], two_l, NT)

    def core_rows(x_):
        return pl.ds(pl.multiple_of(zh * 32 + x_ * 8, 8), 8)

    for d, e in pairs:
        tx, tc = cyc(x, d), c ^ e
        send(cot.at[core_rows(tx)], rc.at[me_xc], s_co.at[d * 2 + e], r_co.at[me_xc], dev(zl, y, tc, zh, tx))
    rc[me_xc] = cot[core_rows(x), :]

    for k in range(Q):
        @pl.when(~(self_d & (k == y)))
        def _():
            arrive(rd.at[k], s_rd.at[k], r_rd.at[k], dev(zl, k, c, zh, y))
    fold(rd, pby, Q)
    for d in range(1, Q):
        tz = cyc(zl, d)
        send(pby.at[tz], rdb.at[zl], s_rdb.at[d], r_rdb.at[zl], dev(tz, y, c, zh, x))
    rdb[zl] = pby[zl]

    for d, e in pairs:
        sx, sc = cyc(x, -d), c ^ e
        i = sx * 2 + sc
        arrive(rc.at[i], s_co.at[d * 2 + e], r_co.at[i], dev(zl, y, sc, zh, sx))
    e0 = (rc[0] + rc[2]) + (rc[4] + rc[6])
    e1 = (rc[1] + rc[3]) + (rc[5] + rc[7])
    both = jnp.where(lane((8, LANES)) < 64, e0, e1)
    et[...] = jnp.concatenate([both] * 16, axis=0).T
    for fh in range(2):
        for z in range(NZ):
            for f in range(HF):
                at = fh * 64 + z * 32 + f * 8
                core_ref[fh * HF + f, z] = jnp.where(c == 0, et[at:at + 4, 0:8], et[at + 4:at + 8, 0:8])

    outputs[3].start()

    for k in range(Q):
        @pl.when(~(self_b & (k == zh)))
        def _():
            arrive(rb.at[k], s_rb.at[k], r_rb.at[k], dev(zh, y, c, k, x))
    unfold(rb, gx_ref, 1.0 / (NF * NZ * NY))
    outputs[1].start()

    for d in range(1, Q):
        sz = cyc(zl, -d)
        arrive(rdb.at[sz], s_rdb.at[d], r_rdb.at[sz], dev(sz, y, c, zh, x))
    unfold(rdb, gy_ref, 1.0 / (NF * NZ * RANK))
    outputs[2].start()

    for copy in outputs:
        copy.wait()
    for copy in sends:
        copy.wait_send()
    for same, copy in late:
        @pl.when(~same)
        def _():
            copy.wait_send()


def place(a, b, c, d, ao, bo, co, do, av, bv, cv, dv, sem):
    into = [pltpu.make_async_copy(src, dst, sem.at[i]) for i, (src, dst) in enumerate([(a, av), (b, bv), (c, cv), (d, dv)])]
    out = [
        pltpu.make_async_copy(src, dst, sem.at[4 + i]) for i, (src, dst) in enumerate([(av, ao), (bv, bo), (cv, co), (dv, do)])
    ]
    for copy in into:
        copy.start()
    for first, second in zip(into, out):
        first.wait()
        second.start()
    for copy in out:
        copy.wait()


def shards(fields, diffusivity, velocity, coupling, basis_x, basis_y):
    vm = lambda *shape: pltpu.VMEM(shape, F32)
    dma = lambda n: pltpu.SemaphoreType.DMA((n,))
    hspec = pl.BlockSpec(memory_space=pl.ANY)
    sm = lambda *shape: pltpu.SMEM(shape, F32)
    scratch = [
        vm(NF, NZ, XR, YC), vm(XR, YC), vm(XR, YC), vm(NF, NZ, 4, 8), dma(4),
        vm(NF, NZ, XR, YC), sm(NF), sm(2, NF), sm(NF, NF),
        pltpu.VMEM((NX, RANK), BF16), pltpu.VMEM((NY, RANK), BF16), dma(6),
        vm(NF * NZ, ROWS, LANES), vm(XR, LANES), vm(XR, LANES), vm(ROWS, LANES), vm(ROWS, LANES),
        vm(NF, NZ, ROWS, LANES), vm(NF, NZ, ROWS, LANES), vm(NF, NZ, ROWS, LANES), vm(2, NF, NZ, ROWS, LANES),
        vm(NF, XR, LANES),
        vm(2 * Q, HF, XR, LANES), vm(2 * Q, HF, XR, LANES),
        vm(Q, 2, YC, LANES), vm(2 * Q, YC, LANES), vm(Q, 16, LANES), vm(Q, 16, LANES),
        vm(Q, Q, HF, 8, LANES), vm(Q, Q, HF, 8, LANES), vm(Q, HF, 8, LANES),
        vm(Q, HF, 8, LANES), vm(HF, 8, LANES),
        vm(Q, HF, 8, LANES), vm(Q, HF, 8, LANES), vm(Q, HF, 8, LANES), vm(Q, HF, 8, LANES),
        vm(Q, YC, LANES), vm(Q, YC, LANES), vm(Q, 16, LANES), vm(Q, 16, LANES),
        vm(RANK, LANES), vm(2 * Q, 8, LANES), vm(LANES, LANES),
        pltpu.VMEM((RANK, 2 * XR), BF16), pltpu.VMEM((RANK, 256), BF16),
        dma(9), dma(9), dma(8), dma(8), dma(8), dma(8), dma(4), dma(4), dma(4), dma(4), dma(4), dma(4), dma(4), dma(4), dma(4), dma(4), dma(4), dma(4),
        dma(8), dma(8), dma(4), dma(4), dma(4), dma(4), dma(4), dma(4), dma(8), dma(8),
    ]
    shapes = (
        jax.ShapeDtypeStruct((NF, NZ, XR, YC), F32),
        jax.ShapeDtypeStruct((XR, YC), F32),
        jax.ShapeDtypeStruct((XR, YC), F32),
        jax.ShapeDtypeStruct((NF, NZ, 4, 8), F32),
    )
    parts = pl.pallas_call(
        kernel,
        out_shape=shapes,
        in_specs=[hspec] * 6,
        out_specs=(hspec,) * 4,
        scratch_shapes=scratch,
        compiler_params=pltpu.CompilerParams(
            collective_id=0, has_side_effects=True, vmem_limit_bytes=63 * 1024 * 1024
        ),
    )(fields, diffusivity, velocity, coupling, basis_x, basis_y)
    state, gram_x, gram_y, core = pl.pallas_call(
        place,
        out_shape=shapes,
        in_specs=[hspec] * 4,
        out_specs=(hspec,) * 4,
        scratch_shapes=[vm(NF, NZ, XR, YC), vm(XR, YC), vm(XR, YC), vm(NF, NZ, 4, 8), dma(8)],
        compiler_params=pltpu.CompilerParams(vmem_limit_bytes=63 * 1024 * 1024),
    )(*parts)
    return state, gram_x, gram_y.T, core


def solution(mesh):
    in_specs = (P(None, None, "sim", ("grp", "gz")), P(), P(), P(), P(), P())
    out_specs = (
        P(None, None, "sim", ("grp", "gz")),
        P("sim", ("grp", "gz")),
        P(("grp", "gz"), "sim"),
        P(None, None, "sim", ("grp", "gz")),
    )
    return jax.shard_map(shards, mesh=mesh, in_specs=in_specs, out_specs=out_specs, check_vma=False)
```
